32 devices in a mesh: dp: 8 (over z, x), mp: 4 (over y, core).
Axes of the slice: x: 2, y: 2, z: 4, core: 2. Of those that a mesh axis runs over, the one named last changes fastest.
Arguments:
- hidden: bfloat16 [128, 4096], P('dp'), may hold values from -6 to 6
- wq_direct: bfloat16 [4096, 2048], P(None, 'mp'), may hold values from -0.09375 to 0.09375
- wkv_direct: bfloat16 [2, 4096, 2048], P(None, None, 'mp'), may hold values from -0.09375 to 0.09375
- wo_direct: bfloat16 [2048, 4096], P(None, 'mp'), may hold values from -0.125 to 0.125
- kv_cache: bfloat16 [2, 128, 32, 2048], P(None, 'dp', None, 'mp'), may hold values from -6 to 6
- parent: int32 [128], P('dp'), may hold values from 0 to 15
- lengths: int32 [128], P('dp'), may hold values from 1 to 32
- cand_embed: bfloat16 [128, 32, 4096], P('dp', None, 'mp'), may hold values from -6 to 6
- source: bfloat16 [8, 8, 4096], P('dp', None, 'mp'), may hold values from -6 to 6
- enc_qkv: bfloat16 [3, 4096, 2048], P(None, 'dp', 'mp'), may hold values from -0.09375 to 0.09375
- enc_out: bfloat16 [2048, 4096], P('dp', 'mp'), may hold values from -0.125 to 0.125
- cross_q: bfloat16 [4096, 2048], P('dp', 'mp'), may hold values from -0.09375 to 0.09375
- cross_kv: bfloat16 [2, 4096, 2048], P(None, 'dp', 'mp'), may hold values from -0.09375 to 0.09375
- cross_out: bfloat16 [2048, 4096], P('dp', 'mp'), may hold values from -0.125 to 0.125
- w_direct: bfloat16 [4096], P('mp'), may hold values from -0.09375 to 0.09375
- w_channel: bfloat16 [4096], P('mp'), may hold values from -0.09375 to 0.09375
- target_shard: int32 [128], P('dp'), may hold values from 0 to 7, as said below
Outputs:
- direct_state: bfloat16 [128, 4096], P('dp', 'mp')
- rerank_score: float32 [128], P('dp')
- channel_score: float32 [128], P('dp')
The draws below stay inside these ranges and needn't reach their ends.
Inputs may be any that keep to these rules, and one draw needn't show every extreme that they name: `target_shard`: every shard receives exactly one candidate of each beam index; a device sends exactly 2 of its candidates to each shard that it sends to.
All inputs are finite; a program needn't handle non-finite values.
Results may differ from the reference program's by a relative error of at most 0.0075.
Values may be sent and summed in bfloat16 or wider, within the bound.
No kernel may reach another device: no remote copies, remote signals or barrier semaphores. Data moves between devices by JAX's collectives and lax.ppermute only.
A program may use at most 128 MiB of HBM per device.

```python
import math
import jax
import jax.numpy as jnp
from jax import lax

D = 4096
HD = 64
BEAMS = 16
LEN = 32
SRC_LEN = 8
HW = 2048
SOURCES = 8
CANDS = 128
N_DP = 8


def draw_target_shard(key, part):
    spread = min(BEAMS, N_DP)
    order = jax.random.permutation(jax.random.fold_in(key, 11), N_DP).astype(jnp.int32)
    values = jnp.arange(N_DP, dtype=jnp.int32)
    rank_of = jnp.zeros((N_DP,), jnp.int32).at[order].set(values)
    special = (values == N_DP - 1) | (values == 1) | (values == N_DP // 2)
    priority = rank_of + N_DP * (1 - special.astype(jnp.int32))
    chosen = jnp.argsort(priority, stable=True)[:spread].astype(jnp.int32)
    shuffle = jax.random.permutation(jax.random.fold_in(key, 13), spread).astype(jnp.int32)
    offsets = chosen[shuffle]
    cand_index = jnp.arange(BEAMS * N_DP, dtype=jnp.int32)
    return ((cand_index // BEAMS + offsets[cand_index % BEAMS % spread]) % N_DP).astype(jnp.int32)


def place_ends(result, stream_key, low, largest):
    index_at = [jax.random.randint(jax.random.fold_in(stream_key, axis), (), 0, length) for axis, length in enumerate(result.shape)]
    longest = result.shape.index(max(result.shape))
    next_to = index_at[:longest] + [(index_at[longest] + 1) % result.shape[longest]] + index_at[longest + 1:]
    return result.at[tuple(index_at)].set(low).at[tuple(next_to)].set(largest)


def block_scale(stream_key, dims, split, low, top_value):
    def one(axis_at, parts):
        steps = jax.random.uniform(jax.random.fold_in(jax.random.fold_in(stream_key, 6), axis_at), (parts,), jnp.float32, low / len(split), top_value / len(split))
        return jnp.repeat(jnp.exp(steps), dims[axis_at] // parts).reshape((-1,) + (1,) * (len(dims) - axis_at - 1))

    loudness = one(*split[0])
    for cut in split[1:]:
        loudness = loudness * one(*cut)
    return loudness


def bell_draw(stream_key, shape, width, bound, split=(), held_as=jnp.bfloat16):
    loudness = block_scale(stream_key, shape, split, -0.22, 0.18) if split else 1.0
    drawn = jax.random.normal(stream_key, shape, jnp.float32) * width * loudness
    return jnp.minimum(jnp.maximum(drawn, -bound), bound).astype(held_as)


def setup_inputs(seed: int = 0) -> dict:
    splits = jax.random.split(jax.random.key(seed), 18)
    hidden = bell_draw(splits[0], (CANDS, D), 1.0, 6.0, ((0, 8),))
    wq_direct = bell_draw(splits[1], (D, HW), D ** -0.5, 0.09375, ((1, 4),))
    wkv_direct = bell_draw(splits[2], (2, D, HW), D ** -0.5, 0.09375, ((2, 4),))
    wo_direct = bell_draw(splits[3], (HW, D), HW ** -0.5, 0.125, ((1, 4),))
    kv_cache = bell_draw(splits[4], (2, CANDS, LEN, HW), 1.0, 6.0, ((1, 8), (3, 4)))
    parent = place_ends(jax.random.randint(splits[5], (CANDS,), 0, BEAMS), jax.random.fold_in(splits[5], 1), 0, BEAMS - 1).astype(jnp.int32)
    lengths = place_ends(jax.random.randint(splits[6], (CANDS,), 1, LEN + 1), jax.random.fold_in(splits[6], 1), 1, LEN).astype(jnp.int32)
    cand_embed = bell_draw(splits[7], (CANDS, LEN, D), 1.0, 6.0, ((0, 8), (2, 4)))
    source = bell_draw(splits[8], (SOURCES, SRC_LEN, D), 1.0, 6.0, ((0, 8), (2, 4)))
    enc_qkv = bell_draw(splits[9], (3, D, HW), D ** -0.5, 0.09375, ((1, 8), (2, 4)))
    enc_out = bell_draw(splits[10], (HW, D), HW ** -0.5, 0.125, ((0, 8), (1, 4)))
    cross_q = bell_draw(splits[11], (D, HW), D ** -0.5, 0.09375, ((0, 8), (1, 4)))
    cross_kv = bell_draw(splits[12], (2, D, HW), D ** -0.5, 0.09375, ((1, 8), (2, 4)))
    cross_out = bell_draw(splits[13], (HW, D), HW ** -0.5, 0.125, ((0, 8), (1, 4)))
    w_direct = bell_draw(splits[14], (D,), D ** -0.5, 0.09375, ((0, 4),))
    w_channel = bell_draw(splits[15], (D,), D ** -0.5, 0.09375, ((0, 4),))
    target_shard = draw_target_shard(jax.random.fold_in(splits[17], 71), 0)
    return {"hidden": hidden, "wq_direct": wq_direct, "wkv_direct": wkv_direct, "wo_direct": wo_direct, "kv_cache": kv_cache, "parent": parent, "lengths": lengths, "cand_embed": cand_embed, "source": source, "enc_qkv": enc_qkv, "enc_out": enc_out, "cross_q": cross_q, "cross_kv": cross_kv, "cross_out": cross_out, "w_direct": w_direct, "w_channel": w_channel, "target_shard": target_shard}


EPSILON = 1e-06

def attend(queries, keys, values, valid):
    group_n, query_n, columns = queries.shape
    key_n = keys.shape[1]
    head_n = columns // HD
    query_heads = queries.reshape(group_n, query_n, head_n, HD).astype(jnp.float32)
    key_heads = keys.reshape(group_n, key_n, head_n, HD).astype(jnp.float32)
    value_heads = values.reshape(group_n, key_n, head_n, HD).astype(jnp.float32)
    scores = jnp.einsum('bqhd,bkhd->bhqk', query_heads, key_heads) / math.sqrt(HD)
    scores = jnp.where(valid[:, None, None, :], scores, -1e+30)
    weights = jax.nn.softmax(scores, axis=-1).astype(jnp.bfloat16)
    context = jnp.einsum('bhqk,bkhd->bqhd', weights.astype(jnp.float32), value_heads)
    return context.astype(jnp.bfloat16).reshape(group_n, query_n, columns)

def project(rows, matrix):
    return jnp.dot(rows, matrix, preferred_element_type=jnp.float32)

def normalized(values):
    return jnp.sqrt(lax.optimization_barrier(jnp.mean(values * values, axis=-1)) + EPSILON)

def reference(hidden, wq_direct, wkv_direct, wo_direct, kv_cache, parent, lengths, cand_embed, source, enc_qkv, enc_out, cross_q, cross_kv, cross_out, w_direct, w_channel, target_shard):
    cand_index = jnp.arange(CANDS, dtype=jnp.int32)
    parent_row = cand_index // BEAMS * BEAMS + parent
    query_new = project(hidden, wq_direct).astype(jnp.bfloat16)
    key_new = project(hidden, wkv_direct[0]).astype(jnp.bfloat16)
    value_new = project(hidden, wkv_direct[1]).astype(jnp.bfloat16)
    all_keys = jnp.concatenate([kv_cache[0][parent_row], key_new[:, None]], axis=1)
    all_values = jnp.concatenate([kv_cache[1][parent_row], value_new[:, None]], axis=1)
    positions = jnp.arange(LEN, dtype=jnp.int32)
    cache_valid = jnp.concatenate([positions[None, :] < lengths[:, None], jnp.ones((CANDS, 1), dtype=bool)], axis=1)
    context = attend(query_new[:, None], all_keys, all_values, cache_valid)[:, 0]
    new_state = hidden.astype(jnp.float32) + project(context, wo_direct)
    direct_score = lax.optimization_barrier(jnp.sum(new_state * w_direct.astype(jnp.float32), axis=1)) / normalized(new_state)

    def score_source(source_id):
        rows_here = lax.dynamic_slice_in_dim(parent_row, source_id * BEAMS, BEAMS)
        lens_here = lax.dynamic_slice_in_dim(lengths, source_id * BEAMS, BEAMS)
        token_rows = cand_embed[rows_here].reshape(BEAMS * LEN, D)
        enc_queries = project(token_rows, enc_qkv[0]).astype(jnp.bfloat16).reshape(BEAMS, LEN, HW)
        enc_keys = project(token_rows, enc_qkv[1]).astype(jnp.bfloat16).reshape(BEAMS, LEN, HW)
        enc_values = project(token_rows, enc_qkv[2]).astype(jnp.bfloat16).reshape(BEAMS, LEN, HW)
        key_valid = positions[None, :] < lens_here[:, None]
        enc_context = attend(enc_queries, enc_keys, enc_values, key_valid).reshape(BEAMS * LEN, HW)
        summed = token_rows.astype(jnp.float32) + project(enc_context, enc_out)
        memory = (summed / normalized(summed)[:, None]).astype(jnp.bfloat16)
        cross_keys = project(memory, cross_kv[0]).astype(jnp.bfloat16).reshape(BEAMS, LEN, HW)
        cross_values = project(memory, cross_kv[1]).astype(jnp.bfloat16).reshape(BEAMS, LEN, HW)
        own_source = lax.dynamic_index_in_dim(source, source_id, 0, keepdims=False)
        queries_once = project(own_source, cross_q).astype(jnp.bfloat16)
        cross_queries = jnp.broadcast_to(queries_once[None], (BEAMS, SRC_LEN, HW))
        cross_context = attend(cross_queries, cross_keys, cross_values, key_valid).reshape(BEAMS * SRC_LEN, HW)
        source_rows = jnp.broadcast_to(own_source[None].astype(jnp.float32), (BEAMS, SRC_LEN, D)).reshape(BEAMS * SRC_LEN, D)
        decoded = source_rows + project(cross_context, cross_out)
        position_score = lax.optimization_barrier(jnp.sum(decoded * w_channel.astype(jnp.float32), axis=1)) / normalized(decoded)
        return lax.optimization_barrier(jnp.mean(position_score.reshape(BEAMS, SRC_LEN), axis=1))
    cand_channel = lax.map(score_source, jnp.arange(N_DP, dtype=jnp.int32)).reshape(CANDS)
    slot_index = target_shard * BEAMS + cand_index % BEAMS
    channel_score = jnp.zeros((CANDS,), jnp.float32).at[slot_index].set(cand_channel)
    rerank_score = direct_score + cand_channel
    return (new_state.astype(jnp.bfloat16), rerank_score, channel_score)
```

```python
import functools
import math

import jax
import jax.numpy as jnp
from jax import lax
from jax.experimental import pallas as pl
from jax.experimental.pallas import tpu as pltpu
from jax.sharding import PartitionSpec as P

HD = 64
EPSILON = 1e-06
NEG = -1e30
LANES = 128
F32 = jnp.float32
BF16 = jnp.bfloat16


def dot(a, b):
    return jnp.dot(a, b, preferred_element_type=F32)


def after(value, *others):
    return lax.optimization_barrier((value, others))[0]


def copy_kernel(index_ref, in_ref, out_ref):
    out_ref[...] = in_ref[...]


def take_rows(rows, index, axis):
    n = index.shape[0]
    block = rows.shape[:axis] + (1,) + rows.shape[axis + 1 :]
    tail = (0,) * (rows.ndim - axis - 1)
    lead = (0,) * axis
    out_shape = rows.shape[:axis] + (n,) + rows.shape[axis + 1 :]
    return pl.pallas_call(
        copy_kernel,
        grid_spec=pltpu.PrefetchScalarGridSpec(
            num_scalar_prefetch=1,
            grid=(n,),
            in_specs=[pl.BlockSpec(block, lambda i, at: lead + (at[i],) + tail)],
            out_specs=pl.BlockSpec(block, lambda i, at: lead + (i,) + tail),
        ),
        out_shape=jax.ShapeDtypeStruct(out_shape, rows.dtype),
        cost_estimate=pl.CostEstimate(
            flops=0, bytes_accessed=4 * math.prod(out_shape), transcendentals=0
        ),
    )(index, rows)


def enc_kernel(width, span, qkv_ref, live_ref, out_ref):
    rows = qkv_ref.shape[0]
    own = lax.broadcasted_iota(jnp.int32, (rows, rows), 0) // span
    other = lax.broadcasted_iota(jnp.int32, (rows, rows), 1) // span
    valid = (own == other) & (live_ref[...] > 0)
    for head in range(width // HD):
        q, k, v = (
            qkv_ref[:, part * width + head * HD : part * width + (head + 1) * HD]
            for part in range(3)
        )
        scores = lax.dot_general(q, k, (((1,), (1,)), ((), ())), preferred_element_type=F32)
        scores = jnp.where(valid, scores * (1.0 / math.sqrt(HD)), NEG)
        top = jnp.max(scores, axis=1, keepdims=True)
        weights = jnp.exp(scores - top)
        weights = (weights / jnp.sum(weights, axis=1, keepdims=True)).astype(BF16)
        out_ref[:, head * HD : (head + 1) * HD] = dot(weights, v).astype(BF16)


def enc_attention(qkv, live, span):
    rows, width = qkv.shape[0], qkv.shape[1] // 3
    return pl.pallas_call(
        functools.partial(enc_kernel, width, span),
        grid=(rows // LANES,),
        in_specs=[
            pl.BlockSpec((LANES, 3 * width), lambda i: (i, 0)),
            pl.BlockSpec((1, LANES), lambda i: (0, i)),
        ],
        out_specs=pl.BlockSpec((LANES, width), lambda i: (i, 0)),
        out_shape=jax.ShapeDtypeStruct((rows, width), BF16),
        cost_estimate=pl.CostEstimate(
            flops=4 * rows * LANES * width,
            bytes_accessed=8 * rows * width,
            transcendentals=rows * LANES * (width // HD),
        ),
    )(qkv, live)


def cross_kernel(span, query_n, scores_ref, scale_ref, live_ref, values_ref, out_ref):
    pairs, lanes = scores_ref.shape[1:]
    width = values_ref.shape[1]
    cands = lanes // span
    scores = scores_ref[0] * (scale_ref[...] * (1.0 / math.sqrt(HD)))
    live = live_ref[...] > 0
    cand = lax.broadcasted_iota(jnp.int32, (pairs, lanes), 1) // span
    scores = jnp.concatenate(
        [jnp.where((cand == c) & live, scores, NEG) for c in range(cands)], axis=0
    )
    top = jnp.max(scores, axis=1, keepdims=True)
    weights = jnp.exp(scores - top)
    weights = (weights / jnp.sum(weights, axis=1, keepdims=True)).astype(BF16)
    context = dot(weights, values_ref[...])
    heads = pairs // query_n
    head = lax.broadcasted_iota(jnp.int32, (query_n, width), 1) // HD
    for c in range(cands):
        total = jnp.zeros((query_n, width), F32)
        for h in range(heads):
            start = (c * heads + h) * query_n
            total = total + jnp.where(head == h, context[start : start + query_n], 0.0)
        out_ref[c * query_n : (c + 1) * query_n] = total.astype(BF16)


def cross_attention(scores, scale, live, values, span, query_n):
    source_n, pairs, rows = scores.shape
    width = values.shape[1]
    per_source = rows // source_n // LANES
    made = LANES // span * query_n
    return pl.pallas_call(
        functools.partial(cross_kernel, span, query_n),
        grid=(rows // LANES,),
        in_specs=[
            pl.BlockSpec((1, pairs, LANES), lambda i: (i // per_source, 0, i)),
            pl.BlockSpec((1, LANES), lambda i: (0, i)),
            pl.BlockSpec((1, LANES), lambda i: (0, i)),
            pl.BlockSpec((LANES, width), lambda i: (i, 0)),
        ],
        out_specs=pl.BlockSpec((made, width), lambda i: (i, 0)),
        out_shape=jax.ShapeDtypeStruct((rows // LANES * made, width), BF16),
        cost_estimate=pl.CostEstimate(
            flops=4 * rows * pairs * width,
            bytes_accessed=2 * rows * width + 4 * pairs * rows,
            transcendentals=rows * pairs * (LANES // span),
        ),
    )(scores, scale, live, values)


def direct_attend(query, keys, values, valid):
    group_n, columns = query.shape
    key_n, head_n = keys.shape[1], columns // HD
    query_heads = query.reshape(group_n, 1, head_n, HD)
    key_heads = keys.reshape(group_n, key_n, head_n, HD)
    value_heads = values.reshape(group_n, key_n, head_n, HD)
    scores = jnp.einsum(
        "bqhd,bkhd->bhqk", query_heads, key_heads, preferred_element_type=F32
    ) / math.sqrt(HD)
    scores = jnp.where(valid[:, None, None, :], scores, NEG)
    weights = jax.nn.softmax(scores, axis=-1).astype(BF16)
    context = jnp.einsum("bhqk,bkhd->bqhd", weights, value_heads, preferred_element_type=F32)
    return context.astype(BF16).reshape(group_n, columns)


def shards(
    hidden,
    wq_direct,
    wkv_direct,
    wo_direct,
    kv_cache,
    parent,
    lengths,
    cand_embed,
    source,
    enc_qkv,
    enc_out,
    cross_q,
    cross_kv,
    cross_out,
    w_direct,
    w_channel,
    target_shard,
):
    dp_n, mp_n = lax.axis_size("dp"), lax.axis_size("mp")
    side_n = dp_n // mp_n
    line_n = dp_n // side_n
    me, own_mp = lax.axis_index("dp"), lax.axis_index("mp")
    side, line = me % side_n, me // side_n
    beam_n, features = hidden.shape
    span = kv_cache.shape[2]
    query_n = source.shape[1]
    rung = [(i, i - i % side_n + (i + 1) % side_n) for i in range(dp_n)]

    def swap(a):
        return lax.ppermute(a, "dp", rung)

    def ordered(own, got, axis):
        return jnp.where(
            side == 0, jnp.concatenate([own, got], axis), jnp.concatenate([got, own], axis)
        )

    def both(a, axis):
        return ordered(a, swap(a), axis)

    def side_part(a, at):
        width = a.shape[-1] // side_n
        return lax.dynamic_slice_in_dim(a, at * width, width, a.ndim - 1)

    def rung_sum(a):
        a = lax.psum(a, "mp")
        return a + swap(a)

    def hop(a, step, up):
        if up:
            lines = [(k, k + 1) for k in range(step - 1, line_n - 1)]
        else:
            lines = [(k, k - 1) for k in range(1, line_n - step + 1)]
        return lax.ppermute(
            a, "dp", [(s * side_n + i, t * side_n + i) for s, t in lines for i in range(side_n)]
        )

    def line_gather(parts):
        ups, downs = [list(parts)], [list(parts)]
        for step in range(1, line_n):
            next_up, next_down = [], []
            for at in range(len(parts)):
                next_up.append(hop(ups[-1][at], step, True))
                next_down.append(hop(downs[-1][at], step, False))
            ups.append(next_up)
            downs.append(next_down)
        slots = [list(parts)]
        for j in range(1, line_n):
            slots.append(
                [
                    jnp.where(line >= j, up, down)
                    for up, down in zip(ups[j], downs[line_n - j], strict=True)
                ]
            )
        return slots, (ups[-1], downs[-1])

    def spread_dot(blocks, slots):
        total = None
        for j, slot in enumerate(slots):
            block = lax.dynamic_index_in_dim(blocks, (line - j) % line_n, 0, keepdims=False)
            part = dot(block, slot)
            total = part if total is None else total + part
        return total

    qkv_own = jnp.concatenate([side_part(w, side) for w in enc_qkv], axis=1)
    qkv_other = jnp.concatenate([side_part(w, 1 - side) for w in enc_qkv], axis=1)
    qkv_got = swap(qkv_other)
    qkv_slots, sent = line_gather([qkv_own, qkv_got])
    qkv_slots = [ordered(own, got, 0) for own, got in qkv_slots]

    def slab(w):
        return ordered(side_part(w, side), swap(side_part(w, 1 - side)), 0)

    out_slots, sent = line_gather([after(slab(enc_out), sent)])
    value_slots, sent = line_gather([after(slab(cross_kv[1]), sent)])
    last_slots, sent = line_gather([after(slab(cross_out), sent)])
    out_slots, value_slots, last_slots = (
        [s for (s,) in slots] for slots in (out_slots, value_slots, last_slots)
    )

    tokens = take_rows(cand_embed, parent, 0)
    local_width = tokens.shape[2]
    token_rows = both(tokens.reshape(beam_n * span, local_width), 0)
    token_blocks = lax.all_gather(token_rows, "mp", axis=0)
    lens = both(lengths, 0)
    positions = jnp.arange(span, dtype=jnp.int32)
    live = (positions[None, :] < lens[:, None]).astype(jnp.int32).reshape(1, -1)

    sources = lax.all_gather(source[0], "dp", axis=0)
    source_blocks = lax.all_gather(sources, "mp", axis=0)
    source_block = lax.dynamic_index_in_dim(source_blocks, line, 0, keepdims=False)
    source_part = side_part(source_block.reshape(dp_n * query_n, local_width), side)
    queries = lax.psum(dot(source_part, cross_q), "dp").astype(BF16)
    head_n = queries.shape[1] // HD
    mixed = jnp.einsum(
        "rhc,khc->hrk",
        queries.reshape(-1, head_n, HD),
        cross_kv[0].reshape(-1, head_n, HD),
        preferred_element_type=F32,
    ).astype(BF16)
    depth = mixed.shape[2]
    side_heads = head_n // side_n
    mixed = mixed.reshape(side_n, side_heads, line_n, side_n, query_n, depth)
    mixed = mixed.transpose(2, 0, 3, 1, 4, 5).reshape(dp_n, -1, depth)
    mixed = lax.all_to_all(mixed, "dp", split_axis=0, concat_axis=0, tiled=True)
    pairs = side_heads * query_n
    mixed = mixed.reshape(line_n, side_n, side_n * pairs, depth).transpose(0, 2, 1, 3)
    mixed = mixed.reshape(line_n, side_n * pairs, side_n * depth)

    own_start = own_mp * local_width
    hidden_share = lax.dynamic_slice_in_dim(hidden, own_start, local_width, 1).astype(F32)
    query_new = dot(hidden, wq_direct).astype(BF16)
    key_new = dot(hidden, wkv_direct[0]).astype(BF16)
    value_new = dot(hidden, wkv_direct[1]).astype(BF16)
    cache = take_rows(kv_cache, parent, 1)
    all_keys = jnp.concatenate([cache[0], key_new[:, None]], axis=1)
    all_values = jnp.concatenate([cache[1], value_new[:, None]], axis=1)
    cache_valid = jnp.concatenate(
        [positions[None, :] < lengths[:, None], jnp.ones((beam_n, 1), dtype=bool)], axis=1
    )
    context = direct_attend(query_new, all_keys, all_values, cache_valid)
    context = lax.all_gather(context, "mp", axis=1, tiled=True)
    new_state = hidden_share + dot(context, wo_direct)
    squares, direct_dot = lax.psum(
        (
            jnp.sum(new_state * new_state, axis=1),
            jnp.sum(new_state * w_direct.astype(F32), axis=1),
        ),
        "mp",
    )
    direct_score = direct_dot / jnp.sqrt(squares / features + EPSILON)

    qkv = spread_dot(token_blocks, qkv_slots).astype(BF16)
    enc_context = enc_attention(qkv, live, span)
    enc_blocks = lax.all_gather(both(enc_context, 1), "mp", axis=0)
    summed = side_part(token_rows, side).astype(F32) + spread_dot(enc_blocks, out_slots)
    enc_squares = rung_sum(jnp.sum(summed * summed, axis=1))
    scale = 1.0 / jnp.sqrt(enc_squares / features + EPSILON)
    memory_blocks = lax.all_gather(both(summed.astype(BF16), 1), "mp", axis=0)

    scores = None
    for k in range(line_n):
        part = lax.dot_general(
            mixed[k], memory_blocks[k], (((1,), (1,)), ((), ())), preferred_element_type=F32
        )
        scores = part if scores is None else scores + part
    cross_values = (spread_dot(memory_blocks, value_slots) * scale[:, None]).astype(BF16)
    cross_context = cross_attention(
        scores.reshape(side_n, pairs, -1), scale[None, :], live, cross_values, span, query_n
    )
    cross_blocks = lax.all_gather(both(cross_context, 1), "mp", axis=0)
    update = spread_dot(cross_blocks, last_slots)
    rung_source = lax.dynamic_slice_in_dim(sources, line * side_n, side_n, 0)
    rung_source = side_part(rung_source, side).astype(F32)
    decoded = rung_source[:, None] + update.reshape(side_n, beam_n, query_n, -1)
    channel_weight = side_part(w_channel, side).astype(F32)
    sums = jnp.stack(
        [jnp.sum(decoded * decoded, axis=-1), jnp.sum(decoded * channel_weight, axis=-1)]
    )
    dec_squares, dec_dot = rung_sum(sums)
    cand_channel = jnp.mean(dec_dot / jnp.sqrt(dec_squares / features + EPSILON), axis=-1)
    own_channel = lax.dynamic_index_in_dim(cand_channel, side, 0, keepdims=False)

    targets = lax.all_gather(target_shard, "dp", axis=0)
    all_channel = lax.all_gather(own_channel, "dp", axis=0)
    channel_score = jnp.sum(jnp.where(targets == me, all_channel, 0.0), axis=0)
    return (new_state.astype(BF16), direct_score + own_channel, channel_score)


def solution(mesh):
    in_specs = (
        P("dp", None),
        P(None, "mp"),
        P(None, None, "mp"),
        P(None, "mp"),
        P(None, "dp", None, "mp"),
        P("dp"),
        P("dp"),
        P("dp", None, "mp"),
        P("dp", None, "mp"),
        P(None, "dp", "mp"),
        P("dp", "mp"),
        P("dp", "mp"),
        P(None, "dp", "mp"),
        P("dp", "mp"),
        P("mp"),
        P("mp"),
        P("dp"),
    )
    out_specs = (P("dp", "mp"), P("dp"), P("dp"))
    return jax.shard_map(shards, mesh=mesh, in_specs=in_specs, out_specs=out_specs, check_vma=False)
```

```python
import functools
import math

import jax
import jax.numpy as jnp
from jax import lax
from jax.experimental import pallas as pl
from jax.experimental.pallas import tpu as pltpu
from jax.sharding import PartitionSpec as P

HD = 64
EPSILON = 1e-06
NEG = -1e30
LANES = 128
F32 = jnp.float32
BF16 = jnp.bfloat16


def dot(a, b):
    return jnp.dot(a, b, preferred_element_type=F32)


def fence(*values):
    return lax.optimization_barrier(values)


def take_kernel(axis, index_ref, in_ref, out_ref):
    lead = (slice(None),) * axis
    for i in range(index_ref.shape[0]):
        out_ref[lead + (i,)] = in_ref[lead + (index_ref[i],)]


def take_rows(rows, index, axis):
    shape = rows.shape[:axis] + index.shape + rows.shape[axis + 1 :]
    return pl.pallas_call(
        functools.partial(take_kernel, axis),
        in_specs=[
            pl.BlockSpec(memory_space=pltpu.SMEM),
            pl.BlockSpec(memory_space=pltpu.VMEM),
        ],
        out_specs=pl.BlockSpec(memory_space=pltpu.VMEM),
        out_shape=jax.ShapeDtypeStruct(shape, rows.dtype),
        compiler_params=pltpu.CompilerParams(vmem_limit_bytes=16 << 20),
        cost_estimate=pl.CostEstimate(
            flops=0, bytes_accessed=4 * math.prod(shape), transcendentals=0
        ),
    )(index, rows)


def enc_kernel(width, span, qkv_ref, live_ref, out_ref):
    own = lax.broadcasted_iota(jnp.int32, (LANES, LANES), 0) // span
    other = lax.broadcasted_iota(jnp.int32, (LANES, LANES), 1) // span
    same = own == other
    ones = jnp.ones((LANES, HD), BF16)
    for start in range(0, qkv_ref.shape[0], LANES):
        rows = slice(start, start + LANES)
        bias = jnp.where(same & (live_ref[:, rows] > 0), 0.0, NEG)
        for head in range(width // HD):
            q, k, v = (
                qkv_ref[rows, part * width + head * HD : part * width + (head + 1) * HD]
                for part in range(3)
            )
            scores = lax.dot_general(q, k, (((1,), (1,)), ((), ())), preferred_element_type=F32)
            scores = scores * (1.0 / math.sqrt(HD)) + bias
            weights = jnp.exp(scores - jnp.max(scores, axis=1, keepdims=True)).astype(BF16)
            context = dot(weights, v) / dot(weights, ones)
            out_ref[rows, head * HD : (head + 1) * HD] = context.astype(BF16)


def enc_attention(qkv, live, span):
    rows, width = qkv.shape[0], qkv.shape[1] // 3
    block = 2 * LANES
    return pl.pallas_call(
        functools.partial(enc_kernel, width, span),
        grid=(rows // block,),
        in_specs=[
            pl.BlockSpec((block, 3 * width), lambda i: (i, 0)),
            pl.BlockSpec((1, block), lambda i: (0, i)),
        ],
        out_specs=pl.BlockSpec((block, width), lambda i: (i, 0)),
        out_shape=jax.ShapeDtypeStruct((rows, width), BF16),
        cost_estimate=pl.CostEstimate(
            flops=4 * rows * LANES * width,
            bytes_accessed=8 * rows * width,
            transcendentals=rows * LANES * (width // HD),
        ),
    )(qkv, live)


def cross_kernel(span, query_n, scores_ref, scale_ref, live_ref, values_ref, out_ref):
    pairs = scores_ref.shape[0]
    width = values_ref.shape[1]
    cands = LANES // span
    heads = pairs // query_n
    cand = lax.broadcasted_iota(jnp.int32, (pairs, LANES), 1) // span
    head = lax.broadcasted_iota(jnp.int32, (query_n, width), 1) // HD
    for at in range(values_ref.shape[0] // LANES):
        rows = slice(at * LANES, (at + 1) * LANES)
        scores = scores_ref[:, rows] * (scale_ref[:, rows] * (1.0 / math.sqrt(HD)))
        live = live_ref[:, rows] > 0
        scores = jnp.concatenate(
            [jnp.where((cand == c) & live, scores, NEG) for c in range(cands)], axis=0
        )
        weights = jnp.exp(scores - jnp.max(scores, axis=1, keepdims=True))
        weights = (weights / jnp.sum(weights, axis=1, keepdims=True)).astype(BF16)
        context = dot(weights, values_ref[rows])
        for c in range(cands):
            total = jnp.zeros((query_n, width), F32)
            for h in range(heads):
                start = (c * heads + h) * query_n
                total = total + jnp.where(head == h, context[start : start + query_n], 0.0)
            start = (at * cands + c) * query_n
            out_ref[start : start + query_n] = total.astype(BF16)


def cross_attention(scores, scale, live, values, span, query_n):
    pairs, rows = scores.shape
    width = values.shape[1]
    return pl.pallas_call(
        functools.partial(cross_kernel, span, query_n),
        in_specs=[pl.BlockSpec(memory_space=pltpu.VMEM)] * 4,
        out_specs=pl.BlockSpec(memory_space=pltpu.VMEM),
        out_shape=jax.ShapeDtypeStruct((rows // span * query_n, width), BF16),
        compiler_params=pltpu.CompilerParams(vmem_limit_bytes=16 << 20),
        cost_estimate=pl.CostEstimate(
            flops=4 * rows * pairs * width,
            bytes_accessed=2 * rows * width + 4 * pairs * rows,
            transcendentals=rows * pairs * (LANES // span),
        ),
    )(scores, scale, live, values)


def direct_attend(query, keys, values, valid):
    group_n, columns = query.shape
    key_n, head_n = keys.shape[1], columns // HD
    query_heads = query.reshape(group_n, 1, head_n, HD)
    key_heads = keys.reshape(group_n, key_n, head_n, HD)
    value_heads = values.reshape(group_n, key_n, head_n, HD)
    scores = jnp.einsum(
        "bqhd,bkhd->bhqk", query_heads, key_heads, preferred_element_type=F32
    ) / math.sqrt(HD)
    scores = jnp.where(valid[:, None, None, :], scores, NEG)
    weights = jax.nn.softmax(scores, axis=-1).astype(BF16)
    context = jnp.einsum("bhqk,bkhd->bqhd", weights, value_heads, preferred_element_type=F32)
    return context.astype(BF16).reshape(group_n, columns)


class Feed:
    def __init__(self, hop, swap, line_n, shards):
        self.hop, self.swap, self.line_n = hop, swap, line_n
        self.shards, self.group, self.step = list(shards), 0, 0
        self.came = [{(0, 0): s} for s in shards]
        self.crossed = [{} for _ in shards]
        self.fresh = None

    def run(self):
        new = []
        if self.fresh is not None:
            group, step = self.fresh
            for way in (1, -1):
                got = self.swap(self.came[group][way, step], way * step)
                new.append((self.crossed[group], (way, step), got))
            self.fresh = None
        if self.group < len(self.shards):
            came = self.came[self.group]
            for way in (1, -1):
                last = came[(way, self.step) if self.step else (0, 0)]
                new.append((came, (way, self.step + 1), self.hop(last, self.step + 1, way > 0)))
            if self.step == 0:
                got = self.swap(came[0, 0], 0)
                new.append((self.crossed[self.group], (0, 0), got))
            self.fresh = (self.group, self.step + 1)
            self.step += 1
            if self.step == self.line_n - 1:
                self.group, self.step = self.group + 1, 0
        return new

    def advance(self, *values):
        new = self.run()
        arrived, values = fence([got for _, _, got in new], values)
        for (store, key, _), got in zip(new, arrived, strict=True):
            store[key] = got
        return values

    def finish(self, group):
        while len(self.crossed[group]) < 2 * self.line_n - 1:
            self.advance()


def shards(
    hidden,
    wq_direct,
    wkv_direct,
    wo_direct,
    kv_cache,
    parent,
    lengths,
    cand_embed,
    source,
    enc_qkv,
    enc_out,
    cross_q,
    cross_kv,
    cross_out,
    w_direct,
    w_channel,
    target_shard,
):
    dp_n, mp_n = lax.axis_size("dp"), lax.axis_size("mp")
    side_n = dp_n // mp_n
    line_n = dp_n // side_n
    me, own_mp = lax.axis_index("dp"), lax.axis_index("mp")
    side, line = me % side_n, me // side_n
    beam_n, features = hidden.shape
    span, query_n = kv_cache.shape[2], source.shape[1]
    local_width = cand_embed.shape[2]

    def swap(a, steps=0):
        lines = range(max(steps, 0), line_n + min(steps, 0))
        pairs = [(k * side_n + i, k * side_n + (i + 1) % side_n) for k in lines for i in range(side_n)]
        return lax.ppermute(a, "dp", pairs)

    def hop(a, step, up):
        if up:
            lines = [(k, k + 1) for k in range(step - 1, line_n - 1)]
        else:
            lines = [(k, k - 1) for k in range(1, line_n - step + 1)]
        pairs = [(s * side_n + i, t * side_n + i) for s, t in lines for i in range(side_n)]
        return lax.ppermute(a, "dp", pairs)

    def ordered(own, got, axis):
        return jnp.where(
            side == 0, jnp.concatenate([own, got], axis), jnp.concatenate([got, own], axis)
        )

    def side_part(a, at):
        width = a.shape[-1] // side_n
        return lax.dynamic_slice_in_dim(a, at * width, width, a.ndim - 1)

    def slots_of(came, crossed):
        slots = [ordered(came[0, 0], crossed[0, 0], 0)]
        for j in range(1, line_n):
            own, got = (
                jnp.where(line >= j, store[1, j], store[-1, line_n - j])
                for store in (came, crossed)
            )
            slots.append(ordered(own, got, 0))
        return slots

    def spread_dot(blocks, slots):
        total = None
        for j, slot in enumerate(slots):
            block = lax.dynamic_index_in_dim(blocks, (line - j) % line_n, 0, keepdims=False)
            part = dot(block, slot)
            total = part if total is None else total + part
        return total

    def everyone(a):
        return lax.all_gather(a, "mp", axis=0)

    feed = Feed(hop, swap, line_n, [enc_out, cross_kv[1], cross_out])
    unit = (line_n - 1) // 3
    positions = jnp.arange(span, dtype=jnp.int32)

    own = jnp.concatenate([side_part(w, side) for w in enc_qkv], axis=1)
    other = jnp.concatenate([side_part(w, 1 - side) for w in enc_qkv], axis=1)
    came, crossed = {(0, 0): own}, {}

    def stage(step, *values):
        new = []
        if step == 0:
            new.append((crossed, (0, 0), swap(other)))
        for store, hops in ((came, step + 1), (crossed, step)):
            if 1 <= hops < line_n:
                for way in (1, -1):
                    last = store[(way, hops - 1) if hops > 1 else (0, 0)]
                    new.append((store, (way, hops), hop(last, hops, way > 0)))
        arrived, values = fence([got for _, _, got in new], values)
        for (store, key, _), got in zip(new, arrived, strict=True):
            store[key] = got
        return values

    tokens = take_rows(cand_embed, parent, 0).reshape(beam_n * span, local_width)
    source_rows = lax.all_gather(source[0], "mp", axis=1, tiled=True)
    tokens, source_rows = stage(0, tokens, source_rows)

    own_blocks = everyone(tokens)
    tokens_got = swap(tokens)
    lengths_got = swap(lengths)
    source_cut = source_rows.reshape(query_n, dp_n, -1).transpose(1, 0, 2)
    source_cut = lax.all_to_all(source_cut, "dp", split_axis=0, concat_axis=0, tiled=True)
    partial = dot(source_cut.reshape(dp_n * query_n, -1), cross_q)
    partial = partial + swap(partial)
    targets = lax.all_gather(target_shard, "dp", axis=0)
    cache = take_rows(kv_cache, parent, 1)
    tokens_got, partial, targets, cache = stage(1, tokens_got, partial, targets, cache)

    got_blocks = everyone(tokens_got)
    total = partial
    for j in range(1, line_n):
        total = total + lax.ppermute(
            partial, "dp", [(i, (i + j * side_n) % dp_n) for i in range(dp_n)]
        )
    queries = total.astype(BF16)
    query_new = dot(hidden, wq_direct).astype(BF16)
    key_new = dot(hidden, wkv_direct[0]).astype(BF16)
    value_new = dot(hidden, wkv_direct[1]).astype(BF16)
    queries, query_new, key_new, value_new = stage(2, queries, query_new, key_new, value_new)

    head_n = queries.shape[1] // HD
    mixed = jnp.einsum(
        "rhc,khc->rhk",
        queries.reshape(-1, head_n, HD),
        cross_kv[0].reshape(-1, head_n, HD),
        preferred_element_type=F32,
    ).astype(BF16)
    depth = mixed.shape[2]
    pairs = head_n * query_n
    mixed = mixed.reshape(dp_n, query_n, head_n, depth).transpose(0, 2, 1, 3)
    mixed = lax.all_to_all(
        mixed.reshape(dp_n, pairs, depth), "dp", split_axis=0, concat_axis=0, tiled=True
    )
    mixed = mixed.reshape(line_n, side_n, pairs, depth).transpose(0, 2, 1, 3)
    mixed = mixed.reshape(line_n, pairs, side_n * depth)
    all_keys = jnp.concatenate([cache[0], key_new[:, None]], axis=1)
    all_values = jnp.concatenate([cache[1], value_new[:, None]], axis=1)
    cache_valid = jnp.concatenate(
        [positions[None, :] < lengths[:, None], jnp.ones((beam_n, 1), dtype=bool)], axis=1
    )
    context = direct_attend(query_new, all_keys, all_values, cache_valid)
    for step in range(3, line_n - 1):
        stage(step)
    for _ in range(unit):
        context, mixed = feed.advance(context, mixed)
    context, mixed, own_blocks, got_blocks = stage(
        line_n - 1, context, mixed, own_blocks, got_blocks
    )

    def live_of(lens):
        return (positions[None, :] < lens[:, None]).astype(jnp.int32).reshape(1, -1)

    qkv_slots = slots_of(came, crossed)
    qkv_got = spread_dot(got_blocks, qkv_slots).astype(BF16)
    context_got = enc_attention(qkv_got, live_of(lengths_got), span)
    for _ in range(unit):
        (context_got,) = feed.advance(context_got)
    live = live_of(lengths)
    qkv_own = spread_dot(own_blocks, qkv_slots).astype(BF16)
    context_own = enc_attention(qkv_own, live, span)
    enc_context = ordered(context_own, swap(context_got), 1)
    for _ in range(unit):
        (enc_context,) = feed.advance(enc_context)
    enc_blocks = everyone(enc_context)
    for _ in range(unit):
        feed.advance()
    feed.finish(0)
    (enc_blocks,) = fence(enc_blocks)
    summed = tokens.astype(F32) + spread_dot(enc_blocks, slots_of(feed.came[0], feed.crossed[0]))
    summed_sent = summed.astype(BF16)
    for _ in range(unit):
        summed, summed_sent = feed.advance(summed, summed_sent)
    memory_blocks = everyone(summed_sent)
    enc_squares = lax.psum(jnp.sum(summed * summed, axis=1), "mp")
    scale = 1.0 / jnp.sqrt(enc_squares / features + EPSILON)
    for _ in range(2 * unit):
        feed.advance()
    feed.finish(1)
    (context,) = feed.advance(context)

    context = lax.all_gather(context, "mp", axis=1, tiled=True)
    own_start = own_mp * local_width
    hidden_share = lax.dynamic_slice_in_dim(hidden, own_start, local_width, 1).astype(F32)
    new_state = hidden_share + dot(context, wo_direct)
    squares, direct_dot = lax.psum(
        (
            jnp.sum(new_state * new_state, axis=1),
            jnp.sum(new_state * w_direct.astype(F32), axis=1),
        ),
        "mp",
    )
    direct_score = direct_dot / jnp.sqrt(squares / features + EPSILON)
    (memory_blocks,) = fence(memory_blocks)

    scores = None
    for k in range(line_n):
        part = lax.dot_general(
            mixed[k], memory_blocks[k], (((1,), (1,)), ((), ())), preferred_element_type=F32
        )
        scores = part if scores is None else scores + part
    value_slots = slots_of(feed.came[1], feed.crossed[1])
    cross_values = (spread_dot(memory_blocks, value_slots) * scale[:, None]).astype(BF16)
    cross_context = cross_attention(scores, scale[None, :], live, cross_values, span, query_n)
    cross_blocks = everyone(cross_context)
    feed.finish(2)
    update = spread_dot(cross_blocks, slots_of(feed.came[2], feed.crossed[2]))
    decoded = source.astype(F32) + update.reshape(beam_n, query_n, -1)
    sums = jnp.stack(
        [jnp.sum(decoded * decoded, axis=-1), jnp.sum(decoded * w_channel.astype(F32), axis=-1)]
    )
    places = lax.broadcasted_iota(jnp.int32, (dp_n, 1, 1, 1), 0) == me
    dec_squares, dec_dot = lax.psum(jnp.where(places, sums[None], 0.0), ("dp", "mp")).swapaxes(0, 1)
    all_channel = jnp.mean(dec_dot / jnp.sqrt(dec_squares / features + EPSILON), axis=-1)
    own_channel = lax.dynamic_index_in_dim(all_channel, me, 0, keepdims=False)
    channel_score = jnp.sum(jnp.where(targets == me, all_channel, 0.0), axis=0)
    return (new_state.astype(BF16), direct_score + own_channel, channel_score)


def solution(mesh):
    in_specs = (
        P("dp", None),
        P(None, "mp"),
        P(None, None, "mp"),
        P(None, "mp"),
        P(None, "dp", None, "mp"),
        P("dp"),
        P("dp"),
        P("dp", None, "mp"),
        P("dp", None, "mp"),
        P(None, "dp", "mp"),
        P("dp", "mp"),
        P("dp", "mp"),
        P(None, "dp", "mp"),
        P("dp", "mp"),
        P("mp"),
        P("mp"),
        P("dp"),
    )
    out_specs = (P("dp", "mp"), P("dp"), P("dp"))
    return jax.shard_map(shards, mesh=mesh, in_specs=in_specs, out_specs=out_specs, check_vma=False)
```

```python
import functools
import math

import jax
import jax.numpy as jnp
from jax import lax
from jax.experimental import pallas as pl
from jax.experimental.pallas import tpu as pltpu
from jax.sharding import PartitionSpec as P

HD = 64
EPSILON = 1e-06
NEG = -1e30
LANES = 128
F32 = jnp.float32
BF16 = jnp.bfloat16


def dot(a, b):
    return jnp.dot(a, b, preferred_element_type=F32)


def fence(*values):
    return lax.optimization_barrier(values)


def take_kernel(axis, index_ref, in_ref, out_ref):
    lead = (slice(None),) * axis
    for i in range(index_ref.shape[0]):
        out_ref[lead + (i,)] = in_ref[lead + (index_ref[i],)]


def take_rows(rows, index, axis):
    shape = rows.shape[:axis] + index.shape + rows.shape[axis + 1 :]
    return pl.pallas_call(
        functools.partial(take_kernel, axis),
        in_specs=[
            pl.BlockSpec(memory_space=pltpu.SMEM),
            pl.BlockSpec(memory_space=pltpu.VMEM),
        ],
        out_specs=pl.BlockSpec(memory_space=pltpu.VMEM),
        out_shape=jax.ShapeDtypeStruct(shape, rows.dtype),
        compiler_params=pltpu.CompilerParams(vmem_limit_bytes=16 << 20),
        cost_estimate=pl.CostEstimate(
            flops=0, bytes_accessed=4 * math.prod(shape), transcendentals=0
        ),
    )(index, rows)


def enc_kernel(width, span, qkv_ref, live_ref, out_ref):
    own = lax.broadcasted_iota(jnp.int32, (LANES, LANES), 0) // span
    other = lax.broadcasted_iota(jnp.int32, (LANES, LANES), 1) // span
    same = own == other
    ones = jnp.ones((LANES, HD), BF16)
    for start in range(0, qkv_ref.shape[0], LANES):
        rows = slice(start, start + LANES)
        bias = jnp.where(same & (live_ref[:, rows] > 0), 0.0, NEG)
        for head in range(width // HD):
            q, k, v = (
                qkv_ref[rows, part * width + head * HD : part * width + (head + 1) * HD]
                for part in range(3)
            )
            scores = lax.dot_general(q, k, (((1,), (1,)), ((), ())), preferred_element_type=F32)
            scores = scores * (1.0 / math.sqrt(HD)) + bias
            weights = jnp.exp(scores - jnp.max(scores, axis=1, keepdims=True)).astype(BF16)
            context = dot(weights, v) / dot(weights, ones)
            out_ref[rows, head * HD : (head + 1) * HD] = context.astype(BF16)


def enc_attention(qkv, live, span):
    rows, width = qkv.shape[0], qkv.shape[1] // 3
    block = 2 * LANES
    return pl.pallas_call(
        functools.partial(enc_kernel, width, span),
        grid=(rows // block,),
        in_specs=[
            pl.BlockSpec((block, 3 * width), lambda i: (i, 0)),
            pl.BlockSpec((1, block), lambda i: (0, i)),
        ],
        out_specs=pl.BlockSpec((block, width), lambda i: (i, 0)),
        out_shape=jax.ShapeDtypeStruct((rows, width), BF16),
        cost_estimate=pl.CostEstimate(
            flops=4 * rows * LANES * width,
            bytes_accessed=8 * rows * width,
            transcendentals=rows * LANES * (width // HD),
        ),
    )(qkv, live)


def cross_kernel(span, query_n, scores_ref, scale_ref, live_ref, values_ref, out_ref):
    pairs = scores_ref.shape[0]
    width = values_ref.shape[1]
    cands = LANES // span
    heads = pairs // query_n
    cand = lax.broadcasted_iota(jnp.int32, (pairs, LANES), 1) // span
    head = lax.broadcasted_iota(jnp.int32, (query_n, width), 1) // HD
    for at in range(values_ref.shape[0] // LANES):
        rows = slice(at * LANES, (at + 1) * LANES)
        scores = scores_ref[:, rows] * (scale_ref[:, rows] * (1.0 / math.sqrt(HD)))
        live = live_ref[:, rows] > 0
        scores = jnp.concatenate(
            [jnp.where((cand == c) & live, scores, NEG) for c in range(cands)], axis=0
        )
        weights = jnp.exp(scores - jnp.max(scores, axis=1, keepdims=True))
        weights = (weights / jnp.sum(weights, axis=1, keepdims=True)).astype(BF16)
        context = dot(weights, values_ref[rows])
        for c in range(cands):
            total = jnp.zeros((query_n, width), F32)
            for h in range(heads):
                start = (c * heads + h) * query_n
                total = total + jnp.where(head == h, context[start : start + query_n], 0.0)
            start = (at * cands + c) * query_n
            out_ref[start : start + query_n] = total.astype(BF16)


def cross_attention(scores, scale, live, values, span, query_n):
    pairs, rows = scores.shape
    width = values.shape[1]
    return pl.pallas_call(
        functools.partial(cross_kernel, span, query_n),
        in_specs=[pl.BlockSpec(memory_space=pltpu.VMEM)] * 4,
        out_specs=pl.BlockSpec(memory_space=pltpu.VMEM),
        out_shape=jax.ShapeDtypeStruct((rows // span * query_n, width), BF16),
        compiler_params=pltpu.CompilerParams(vmem_limit_bytes=16 << 20),
        cost_estimate=pl.CostEstimate(
            flops=4 * rows * pairs * width,
            bytes_accessed=2 * rows * width + 4 * pairs * rows,
            transcendentals=rows * pairs * (LANES // span),
        ),
    )(scores, scale, live, values)


def direct_attend(query, keys, values, valid):
    group_n, columns = query.shape
    key_n, head_n = keys.shape[1], columns // HD
    query_heads = query.reshape(group_n, 1, head_n, HD)
    key_heads = keys.reshape(group_n, key_n, head_n, HD)
    value_heads = values.reshape(group_n, key_n, head_n, HD)
    scores = jnp.einsum(
        "bqhd,bkhd->bhqk", query_heads, key_heads, preferred_element_type=F32
    ) / math.sqrt(HD)
    scores = jnp.where(valid[:, None, None, :], scores, NEG)
    weights = jax.nn.softmax(scores, axis=-1).astype(BF16)
    context = jnp.einsum("bhqk,bkhd->bqhd", weights, value_heads, preferred_element_type=F32)
    return context.astype(BF16).reshape(group_n, columns)


def shards(
    hidden,
    wq_direct,
    wkv_direct,
    wo_direct,
    kv_cache,
    parent,
    lengths,
    cand_embed,
    source,
    enc_qkv,
    enc_out,
    cross_q,
    cross_kv,
    cross_out,
    w_direct,
    w_channel,
    target_shard,
):
    dp_n, mp_n = lax.axis_size("dp"), lax.axis_size("mp")
    side_n = dp_n // mp_n
    line_n = dp_n // side_n
    me, own_mp = lax.axis_index("dp"), lax.axis_index("mp")
    side, line = me % side_n, me // side_n
    beam_n, features = hidden.shape
    span, query_n = kv_cache.shape[2], source.shape[1]
    local_width = cand_embed.shape[2]
    by_pairs = line_n == 4
    inner = (line == 1) | (line == 2)

    def move(a, pairs):
        return lax.ppermute(
            a, "dp", [(s * side_n + i, t * side_n + i) for s, t in pairs for i in range(side_n)]
        )

    def swap(a):
        return lax.ppermute(
            a, "dp", [(i, i - i % side_n + (i + 1) % side_n) for i in range(dp_n)]
        )

    def near(store):
        if not by_pairs:
            return []
        return [
            (store, "next", move(store["own"], [(0, 1), (1, 0), (2, 3), (3, 2)])),
            (store, "inner", move(store["own"], [(1, 2), (2, 1)])),
        ]

    def far(store):
        if not by_pairs:
            lines = [[k * side_n + i for k in range(line_n)] for i in range(side_n)]
            return [(store, "far", lax.all_gather(store["own"], "dp", axis_index_groups=lines))]
        return [
            (store, "outer", move(store["inner"], [(1, 0), (2, 3)])),
            (store, "inner_last", move(store["next"], [(1, 2), (2, 1)])),
            (store, "outer_last", move(store["next"], [(1, 3), (2, 0)])),
        ]

    def join(store):
        if by_pairs:
            store["far"] = jnp.stack(
                [
                    jnp.where(inner, store["inner"], store["outer"]),
                    jnp.where(inner, store["inner_last"], store["outer_last"]),
                ]
            )

    def cross(store, crossed, *keys):
        return [(crossed, key, swap(store[key])) for key in keys if key in store]

    def settle(made, held, *values):
        places = [(store, key) for store, key, _ in made]
        places += [(store, key) for store, key in held if key in store]
        arrays = [a for _, _, a in made]
        arrays += [store[key] for store, key in held if key in store]
        arrays, values = fence(arrays, values)
        for (store, key), a in zip(places, arrays, strict=True):
            store[key] = a
        return values

    def slots_of(store):
        if not by_pairs:
            return [(k, store["far"][k]) for k in range(line_n)]
        low = line < 2
        return [
            (line, store["own"]),
            (line ^ 1, store["next"]),
        ] + [
            (jnp.where(low, 2 + k, 1 - k), store["far"][k]) for k in range(2) if "far" in store
        ]

    def ordered(own, got, axis):
        return jnp.where(
            side == 0, jnp.concatenate([own, got], axis), jnp.concatenate([got, own], axis)
        )

    def slots_across(store, crossed):
        pairs = zip(slots_of(store), slots_of(crossed), strict=True)
        return [(place, ordered(own, got, 0)) for (place, own), (_, got) in pairs]

    def side_part(a, at):
        width = a.shape[-1] // side_n
        return lax.dynamic_slice_in_dim(a, at * width, width, a.ndim - 1)

    def spread_dot(blocks, slots, total=None):
        for place, slot in slots:
            part = dot(lax.dynamic_index_in_dim(blocks, place, 0, keepdims=False), slot)
            total = part if total is None else total + part
        return total

    def everyone(a):
        return lax.all_gather(a, "mp", axis=0)

    def exchange(a):
        return lax.all_to_all(a, "dp", split_axis=0, concat_axis=0, tiled=True)

    positions = jnp.arange(span, dtype=jnp.int32)

    out, out_other = {"own": enc_out}, {}
    val, val_other = {"own": cross_kv[1]}, {}
    last, last_other = {"own": cross_out}, {}
    qkv_own = jnp.concatenate([side_part(w, side) for w in enc_qkv], axis=1)
    qkv_got = swap(jnp.concatenate([side_part(w, 1 - side) for w in enc_qkv], axis=1))
    out_near = near(out)
    last_near = near(last)
    tokens = take_rows(cand_embed, parent, 0).reshape(beam_n * span, local_width)
    source_rows = lax.all_gather(source[0], "mp", axis=1, tiled=True)
    source_cut = source_rows.reshape(query_n, dp_n, -1).transpose(1, 0, 2)
    source_cut = exchange(source_cut)
    qkv_got, tokens, source_cut = settle(out_near, [], qkv_got, tokens, source_cut)

    both = jnp.zeros((side_n,) + qkv_own.shape, BF16)
    both = lax.dynamic_update_index_in_dim(both, qkv_own, side, 0)
    both = lax.dynamic_update_index_in_dim(both, qkv_got, 1 - side, 0)
    qkv = {"own": both.reshape(-1, both.shape[2])}
    qkv_near = near(qkv)
    tokens_got = swap(tokens)
    own_blocks = everyone(tokens)
    cache = take_rows(kv_cache, parent, 1)
    partial = exchange(dot(source_cut.reshape(dp_n * query_n, -1), cross_q))
    query_new = dot(hidden, wq_direct).astype(BF16)
    key_new = dot(hidden, wkv_direct[0]).astype(BF16)
    value_new = dot(hidden, wkv_direct[1]).astype(BF16)
    bases = [(store, "own") for store in (out, val, last)]
    tokens_got, partial, cache, query_new, key_new, value_new = settle(
        qkv_near + last_near, bases, tokens_got, partial, cache, query_new, key_new, value_new
    )

    qkv_far = far(qkv)
    got_blocks = everyone(tokens_got)
    lengths_got = swap(lengths)
    (lengths_got,) = settle(cross(out, out_other, "own", "next"), bases, lengths_got)
    queries = jnp.sum(partial.reshape(dp_n, query_n, -1), axis=0).astype(BF16)
    queries = exchange(jnp.broadcast_to(queries, (dp_n,) + queries.shape).reshape(dp_n * query_n, -1))
    (queries,) = settle(
        cross(val, val_other, "own") + cross(last, last_other, "own"), [(last, "next")], queries
    )
    last_cross = cross(last, last_other, "next")
    head_n = queries.shape[1] // HD
    mixed = jnp.einsum(
        "rhc,khc->rhk",
        queries.reshape(-1, head_n, HD),
        cross_kv[0].reshape(-1, head_n, HD),
        preferred_element_type=F32,
    ).astype(BF16)
    depth = mixed.shape[2]
    pairs = head_n * query_n
    mixed = mixed.reshape(dp_n, query_n, head_n, depth).transpose(0, 2, 1, 3)
    mixed = exchange(mixed.reshape(dp_n, pairs, depth))
    all_keys = jnp.concatenate([cache[0], key_new[:, None]], axis=1)
    all_values = jnp.concatenate([cache[1], value_new[:, None]], axis=1)
    cache_valid = jnp.concatenate(
        [positions[None, :] < lengths[:, None], jnp.ones((beam_n, 1), dtype=bool)], axis=1
    )
    context = direct_attend(query_new, all_keys, all_values, cache_valid)
    context = lax.all_gather(context, "mp", axis=1, tiled=True)
    own_start = own_mp * local_width
    hidden_share = lax.dynamic_slice_in_dim(hidden, own_start, local_width, 1).astype(F32)
    new_state = hidden_share + dot(context, wo_direct)
    squares, direct_dot = lax.psum(
        (
            jnp.sum(new_state * new_state, axis=1),
            jnp.sum(new_state * w_direct.astype(F32), axis=1),
        ),
        "mp",
    )
    direct_score = direct_dot / jnp.sqrt(squares / features + EPSILON)
    new_state = new_state.astype(BF16)
    early = slots_of(qkv)[:2] if by_pairs else []
    rows_got = spread_dot(got_blocks, early)
    rows_own = spread_dot(own_blocks, early)
    new_state, direct_score, own_blocks, got_blocks, rows_got, rows_own = settle(
        qkv_far + last_cross,
        [(out, "inner"), (out, "next"), (val, "own")],
        new_state,
        direct_score,
        own_blocks,
        got_blocks,
        rows_got,
        rows_own,
    )

    def live_of(lens):
        return (positions[None, :] < lens[:, None]).astype(jnp.int32).reshape(1, -1)

    out_far = far(out)
    join(qkv)
    qkv_slots = slots_of(qkv)[len(early) :]
    rows_got = spread_dot(got_blocks, qkv_slots, rows_got).astype(BF16)
    context_got = enc_attention(rows_got, live_of(lengths_got), span)
    live = live_of(lengths)
    rows_own = spread_dot(own_blocks, qkv_slots, rows_own).astype(BF16)
    context_own = enc_attention(rows_own, live, span)
    context_got, context_own, mixed = settle(
        out_far, [(val, "own")], context_got, context_own, mixed
    )

    join(out)
    context_got = swap(context_got)
    out_cross = cross(out, out_other, "far")
    enc_context = ordered(context_own, context_got, 1)
    (enc_context,) = settle(near(val), [], enc_context)
    enc_blocks = everyone(enc_context)
    val_far = far(val)
    settle(out_cross, [(val, "next")])
    val_cross = cross(val, val_other, "next")
    (enc_blocks,) = fence(enc_blocks)
    summed = tokens.astype(F32) + spread_dot(enc_blocks, slots_across(out, out_other))
    summed_sent = summed.astype(BF16)
    summed, summed_sent = settle(
        val_far, [(last, "inner"), (last, "next")], summed, summed_sent
    )
    memory_blocks = everyone(summed_sent)
    join(val)
    val_cross += cross(val, val_other, "far")
    last_far = far(last)
    enc_squares = lax.psum(jnp.sum(summed * summed, axis=1), "mp")
    scale = 1.0 / jnp.sqrt(enc_squares / features + EPSILON)
    (scale,) = settle(val_cross + last_far, [], scale)
    join(last)
    last_cross = cross(last, last_other, "far")
    (memory_blocks,) = fence(memory_blocks)

    mixed = mixed.reshape(line_n, side_n, pairs, depth).transpose(0, 2, 1, 3)
    mixed = mixed.reshape(line_n, pairs, side_n * depth)

    scores = None
    for k in range(line_n):
        part = lax.dot_general(
            mixed[k], memory_blocks[k], (((1,), (1,)), ((), ())), preferred_element_type=F32
        )
        scores = part if scores is None else scores + part
    cross_values = spread_dot(memory_blocks, slots_across(val, val_other))
    cross_values = (cross_values * scale[:, None]).astype(BF16)
    cross_context = cross_attention(scores, scale[None, :], live, cross_values, span, query_n)
    cross_blocks = everyone(cross_context)
    (cross_blocks,) = settle(last_cross, [], cross_blocks)
    update = spread_dot(cross_blocks, slots_across(last, last_other))
    decoded = source.astype(F32) + update.reshape(beam_n, query_n, -1)
    dec_squares, dec_dot = lax.psum(
        (
            jnp.sum(decoded * decoded, axis=-1).reshape(1, -1),
            jnp.sum(decoded * w_channel.astype(F32), axis=-1).reshape(1, -1),
        ),
        "mp",
    )
    position_score = dec_dot / jnp.sqrt(dec_squares / features + EPSILON)
    own_channel = jnp.mean(position_score.reshape(beam_n, query_n), axis=1)
    shard_ids = lax.broadcasted_iota(jnp.int32, (dp_n, beam_n), 0)
    sent_scores = jnp.where(shard_ids == target_shard[None], own_channel[None], 0.0)
    return (new_state, direct_score + own_channel, jnp.sum(exchange(sent_scores), axis=0))


def solution(mesh):
    in_specs = (
        P("dp", None),
        P(None, "mp"),
        P(None, None, "mp"),
        P(None, "mp"),
        P(None, "dp", None, "mp"),
        P("dp"),
        P("dp"),
        P("dp", None, "mp"),
        P("dp", None, "mp"),
        P(None, "dp", "mp"),
        P("dp", "mp"),
        P("dp", "mp"),
        P(None, "dp", "mp"),
        P("dp", "mp"),
        P("mp"),
        P("mp"),
        P("dp"),
    )
    out_specs = (P("dp", "mp"), P("dp"), P("dp"))
    return jax.shard_map(shards, mesh=mesh, in_specs=in_specs, out_specs=out_specs, check_vma=False)
```

```python
import functools
import math

import jax
import jax.numpy as jnp
from jax import lax
from jax.experimental import pallas as pl
from jax.experimental.pallas import tpu as pltpu
from jax.sharding import PartitionSpec as P

HD = 64
EPSILON = 1e-06
NEG = -1e30
LANES = 128
F32 = jnp.float32
BF16 = jnp.bfloat16


def dot(a, b):
    return jnp.dot(a, b, preferred_element_type=F32)


def fence(*values):
    return lax.optimization_barrier(values)


def take_kernel(axis, index_ref, in_ref, out_ref):
    lead = (slice(None),) * axis
    for i in range(index_ref.shape[0]):
        out_ref[lead + (i,)] = in_ref[lead + (index_ref[i],)]


def take_rows(rows, index, axis):
    shape = rows.shape[:axis] + index.shape + rows.shape[axis + 1 :]
    return pl.pallas_call(
        functools.partial(take_kernel, axis),
        in_specs=[
            pl.BlockSpec(memory_space=pltpu.SMEM),
            pl.BlockSpec(memory_space=pltpu.VMEM),
        ],
        out_specs=pl.BlockSpec(memory_space=pltpu.VMEM),
        out_shape=jax.ShapeDtypeStruct(shape, rows.dtype),
        compiler_params=pltpu.CompilerParams(vmem_limit_bytes=16 << 20),
        cost_estimate=pl.CostEstimate(
            flops=0, bytes_accessed=4 * math.prod(shape), transcendentals=0
        ),
    )(index, rows)


VMEM = pl.BlockSpec(memory_space=pltpu.VMEM)
SMEM = pl.BlockSpec(memory_space=pltpu.SMEM)


def local_call(kernel, inputs, out_shapes, scratch=()):
    return pl.pallas_call(
        kernel,
        in_specs=[SMEM] + [VMEM] * (len(inputs) - 1),
        out_specs=[VMEM] * len(out_shapes),
        out_shape=[jax.ShapeDtypeStruct(*shape) for shape in out_shapes],
        scratch_shapes=[pltpu.VMEM(*shape) for shape in scratch],
        compiler_params=pltpu.CompilerParams(vmem_limit_bytes=36 << 20),
        cost_estimate=pl.CostEstimate(flops=1000, bytes_accessed=1000, transcendentals=0),
    )(*inputs)


def tile_of(n):
    return 256 if n % 256 == 0 else n


def for_tiles(n, body):
    tile = tile_of(n)
    if tile == n:
        body(pl.ds(0, n))
        return

    def step(i, carry):
        body(pl.ds(pl.multiple_of(i * tile, tile), tile))
        return carry

    lax.fori_loop(0, n // tile, step, 0)


def spread_tile(at_ref, blocks_ref, slots, rows, cols, fold_at=0):
    here = at_ref[0] == 0
    total = None
    for j, parts in enumerate(slots):
        place = at_ref[j + 2]
        loaded = [load_part(ref, k, cols, fold_at) for ref, k, *_ in parts]
        if len(parts[0]) == 3:
            loaded = [jnp.where(at_ref[1] == 1, loaded[0], parts[0][2][:, cols])]
        if len(loaded) == 2:
            own, got = loaded
            loaded = [jnp.where(here, own, got), jnp.where(here, got, own)]
        depth = loaded[0].shape[0]
        for k, weights in enumerate(loaded):
            part = dot(blocks_ref[place, rows, k * depth : (k + 1) * depth], weights)
            total = part if total is None else total + part
    return total


def load_part(ref, index, cols, fold_at):
    lead = () if index is None else (index,)
    part = ref[lead + (slice(None), cols)]
    if fold_at:
        right = pl.ds(cols.start + fold_at, cols.size)
        part = jnp.concatenate([part, ref[lead + (slice(None), right)]], axis=0)
    return part


def bind(keys, *refs):
    pairs = [key if isinstance(key[0], tuple) else (key,) for key in keys]
    return [[(refs[key[0]], key[1], *(refs[k] for k in key[2:])) for key in parts] for parts in pairs]


def enc_kernel(keys, slot_n, span, at_ref, blocks_ref, live_ref, *refs):
    slots = bind(keys, *refs[:slot_n])
    out_ref, qkv_ref = refs[slot_n:]
    total_rows, width = out_ref.shape

    def project(rows):
        def columns(cols):
            qkv_ref[rows, cols] = spread_tile(at_ref, blocks_ref, slots, rows, cols).astype(BF16)

        for_tiles(qkv_ref.shape[1], columns)

    for_tiles(total_rows, project)
    own = lax.broadcasted_iota(jnp.int32, (LANES, LANES), 0) // span
    other = lax.broadcasted_iota(jnp.int32, (LANES, LANES), 1) // span
    same = own == other
    ones = jnp.ones((LANES, HD), BF16)
    for start in range(0, total_rows, LANES):
        rows = slice(start, start + LANES)
        bias = jnp.where(same & (live_ref[:, rows] > 0), 0.0, NEG)
        for head in range(width // HD):
            q, k, v = (
                qkv_ref[rows, part * width + head * HD : part * width + (head + 1) * HD]
                for part in range(3)
            )
            scores = lax.dot_general(q, k, (((1,), (1,)), ((), ())), preferred_element_type=F32)
            scores = scores * (1.0 / math.sqrt(HD)) + bias
            weights = jnp.exp(scores - jnp.max(scores, axis=1, keepdims=True)).astype(BF16)
            context = dot(weights, v) / dot(weights, ones)
            out_ref[rows, head * HD : (head + 1) * HD] = context.astype(BF16)


def enc_attention(at, blocks, live, keys, slots, span):
    rows, triple = blocks.shape[1], slots[0].shape[-1]
    return local_call(
        functools.partial(enc_kernel, keys, len(slots), span),
        (at, blocks, live, *slots),
        [((rows, triple // 3), BF16)],
        [((rows, triple), BF16)],
    )[0]


def out_kernel(keys, slot_n, at_ref, blocks_ref, tokens_ref, *refs):
    slots = bind(keys, *refs[:slot_n])
    summed_ref, squares_ref = refs[slot_n:]
    squares_ref[...] = jnp.zeros_like(squares_ref)

    def row_tile(rows):
        def columns(cols):
            summed = spread_tile(at_ref, blocks_ref, slots, rows, cols)
            summed = summed + tokens_ref[rows, cols].astype(F32)
            summed_ref[rows, cols] = summed.astype(BF16)
            squares_ref[rows] += jnp.sum(summed * summed, axis=1, keepdims=True)

        for_tiles(summed_ref.shape[1], columns)

    for_tiles(summed_ref.shape[0], row_tile)


def encode_out(at, blocks, tokens, keys, slots):
    return local_call(
        functools.partial(out_kernel, keys, len(slots)),
        (at, blocks, tokens, *slots),
        [(tokens.shape, BF16), ((tokens.shape[0], 1), F32)],
    )


def decode_kernel(keys, slot_n, span, query_n, at_ref, blocks_ref, mixed_ref, column_ref, row_ref, live_ref, *refs):
    slots = bind(keys, *refs[:slot_n])
    out_ref, values_ref, scores_ref = refs[slot_n:]
    total_rows, width = values_ref.shape

    def project(rows):
        def columns(cols):
            values = spread_tile(at_ref, blocks_ref, slots, rows, cols, width) * column_ref[rows]
            values_ref[rows, cols] = values.astype(BF16)

        for_tiles(width, columns)

    for_tiles(total_rows, project)
    total = None
    for k in range(blocks_ref.shape[0]):
        part = lax.dot_general(
            mixed_ref[k], blocks_ref[k], (((1,), (1,)), ((), ())), preferred_element_type=F32
        )
        total = part if total is None else total + part
    scores_ref[...] = total * (row_ref[...] * (1.0 / math.sqrt(HD)))
    pairs = scores_ref.shape[0]
    cands = LANES // span
    heads = pairs // query_n
    cand = lax.broadcasted_iota(jnp.int32, (pairs, LANES), 1) // span
    head = lax.broadcasted_iota(jnp.int32, (query_n, width), 1) // HD
    for at in range(total_rows // LANES):
        rows = slice(at * LANES, (at + 1) * LANES)
        scores = scores_ref[:, rows]
        live = live_ref[:, rows] > 0
        scores = jnp.concatenate(
            [jnp.where((cand == c) & live, scores, NEG) for c in range(cands)], axis=0
        )
        weights = jnp.exp(scores - jnp.max(scores, axis=1, keepdims=True))
        weights = (weights / jnp.sum(weights, axis=1, keepdims=True)).astype(BF16)
        context = dot(weights, values_ref[rows])
        made = []
        for c in range(cands):
            chosen = jnp.zeros((query_n, width), F32)
            for h in range(heads):
                start = (c * heads + h) * query_n
                chosen = chosen + jnp.where(head == h, context[start : start + query_n], 0.0)
            made.append(chosen)
        made = jnp.concatenate(made, axis=0).astype(BF16)
        out_ref[at * cands * query_n : (at + 1) * cands * query_n] = made


def decode(at, blocks, mixed, scale, live, keys, slots, span, query_n):
    rows, width = blocks.shape[1], slots[0].shape[-1] // 2
    return local_call(
        functools.partial(decode_kernel, keys, len(slots), span, query_n),
        (at, blocks, mixed, scale, scale.reshape(1, -1), live, *slots),
        [((rows // span * query_n, width), BF16)],
        [((rows, width), BF16), ((mixed.shape[1], rows), F32)],
    )[0]


def last_kernel(keys, slot_n, at_ref, blocks_ref, source_ref, weight_ref, *refs):
    slots = bind(keys, *refs[:slot_n])
    squares_ref, dots_ref = refs[slot_n:]
    squares_ref[...] = jnp.zeros_like(squares_ref)
    dots_ref[...] = jnp.zeros_like(dots_ref)
    total_rows, query_n = squares_ref.shape[0], source_ref.shape[0]

    def columns(cols):
        update = spread_tile(at_ref, blocks_ref, slots, pl.ds(0, total_rows), cols)
        source = source_ref[:, cols].astype(F32)
        decoded = update + jnp.concatenate([source] * (total_rows // query_n), axis=0)
        squares_ref[...] += jnp.sum(decoded * decoded, axis=1, keepdims=True)
        weighted = decoded * weight_ref[:, cols].astype(F32)
        dots_ref[...] += jnp.sum(weighted, axis=1, keepdims=True)

    for_tiles(source_ref.shape[1], columns)


def decode_out(at, blocks, source, weight, keys, slots):
    column = ((blocks.shape[1], 1), F32)
    return local_call(
        functools.partial(last_kernel, keys, len(slots)),
        (at, blocks, source, weight, *slots),
        [column, column],
    )


def direct_kernel(span, live_ref, hidden_ref, wq_ref, wkv_ref, cache_ref, out_ref):
    beams, width = out_ref.shape
    heads = width // HD
    hidden = hidden_ref[...]
    query, key, value = (
        dot(hidden, weights).astype(BF16) for weights in (wq_ref[...], wkv_ref[0], wkv_ref[1])
    )
    column_head = lax.broadcasted_iota(jnp.int32, (beams, width), 1) // HD
    spread = jnp.concatenate(
        [jnp.where(column_head == h, query.astype(F32), 0.0) for h in range(heads)], axis=0
    ).astype(BF16)
    rows = heads * beams

    def product(keys):
        return lax.dot_general(spread, keys, (((1,), (1,)), ((), ())), preferred_element_type=F32)

    def beam_of(shape, axis, n):
        index = lax.broadcasted_iota(jnp.int32, shape, axis)
        return index % beams if axis == 0 else index // n

    old = (rows, beams * span)
    valid = (beam_of(old, 0, 1) == beam_of(old, 1, span)) & (live_ref[...] > 0)
    scores = jnp.where(valid, product(cache_ref[0]) * (1.0 / math.sqrt(HD)), NEG)
    new = (rows, beams)
    fresh = beam_of(new, 0, 1) == beam_of(new, 1, 1)
    scores_new = jnp.where(fresh, product(key) * (1.0 / math.sqrt(HD)), NEG)
    top = jnp.maximum(
        jnp.max(scores, axis=1, keepdims=True), jnp.max(scores_new, axis=1, keepdims=True)
    )
    weights, weights_new = jnp.exp(scores - top), jnp.exp(scores_new - top)
    total = jnp.sum(weights, axis=1, keepdims=True) + jnp.sum(weights_new, axis=1, keepdims=True)
    context = dot((weights / total).astype(BF16), cache_ref[1])
    context = context + dot((weights_new / total).astype(BF16), value)
    chosen = jnp.zeros((beams, width), F32)
    for h in range(heads):
        chosen = chosen + jnp.where(column_head == h, context[h * beams : (h + 1) * beams], 0.0)
    out_ref[...] = chosen.astype(BF16)


def direct_context(live, hidden, wq, wkv, cache, span):
    return pl.pallas_call(
        functools.partial(direct_kernel, span),
        in_specs=[VMEM] * 5,
        out_specs=VMEM,
        out_shape=jax.ShapeDtypeStruct((hidden.shape[0], wq.shape[1]), BF16),
        compiler_params=pltpu.CompilerParams(vmem_limit_bytes=36 << 20),
        cost_estimate=pl.CostEstimate(flops=1000, bytes_accessed=1000, transcendentals=0),
    )(live, hidden, wq, wkv, cache)


def state_kernel(context_ref, wo_ref, hidden_ref, weight_ref, state_ref, squares_ref, dots_ref):
    state = hidden_ref[...].astype(F32) + dot(context_ref[...], wo_ref[...])
    state_ref[...] = state.astype(BF16)
    squares_ref[...] = jnp.sum(state * state, axis=1, keepdims=True)
    dots_ref[...] = jnp.sum(state * weight_ref[...].astype(F32), axis=1, keepdims=True)


def direct_state(context, wo, hidden, weight):
    column = jax.ShapeDtypeStruct((hidden.shape[0], 1), F32)
    return pl.pallas_call(
        state_kernel,
        in_specs=[VMEM] * 4,
        out_specs=[VMEM] * 3,
        out_shape=[jax.ShapeDtypeStruct(hidden.shape, BF16), column, column],
        compiler_params=pltpu.CompilerParams(vmem_limit_bytes=36 << 20),
        cost_estimate=pl.CostEstimate(flops=1000, bytes_accessed=1000, transcendentals=0),
    )(context, wo, hidden, weight)


def shards(
    hidden,
    wq_direct,
    wkv_direct,
    wo_direct,
    kv_cache,
    parent,
    lengths,
    cand_embed,
    source,
    enc_qkv,
    enc_out,
    cross_q,
    cross_kv,
    cross_out,
    w_direct,
    w_channel,
    target_shard,
):
    dp_n, mp_n = lax.axis_size("dp"), lax.axis_size("mp")
    side_n = dp_n // mp_n
    line_n = dp_n // side_n
    me, own_mp = lax.axis_index("dp"), lax.axis_index("mp")
    side, line = me % side_n, me // side_n
    beam_n, features = hidden.shape
    span, query_n = kv_cache.shape[2], source.shape[1]
    local_width = cand_embed.shape[2]
    by_pairs = line_n == 4
    inner = (line == 1) | (line == 2)

    def move(a, pairs):
        return lax.ppermute(
            a, "dp", [(s * side_n + i, t * side_n + i) for s, t in pairs for i in range(side_n)]
        )

    def swap(a):
        return lax.ppermute(
            a, "dp", [(i, i - i % side_n + (i + 1) % side_n) for i in range(dp_n)]
        )

    def to_next(a):
        return move(a, [(0, 1), (1, 0), (2, 3), (3, 2)])

    def to_inner(a):
        return move(a, [(1, 2), (2, 1)])

    def far(own, of_next, of_inner):
        if not by_pairs:
            lines = [[k * side_n + i for k in range(line_n)] for i in range(side_n)]
            return [lax.all_gather(own, "dp", axis_index_groups=lines)]
        return [
            move(of_inner, [(1, 0), (2, 3)]),
            move(of_next, [(1, 2), (2, 1)]),
            move(of_next, [(1, 3), (2, 0)]),
        ]

    def join(of_inner, made):
        if not by_pairs:
            return made[0]
        outer, inner_last, outer_last = made
        return jnp.stack(
            [jnp.where(inner, of_inner, outer), jnp.where(inner, inner_last, outer_last)]
        )

    low = line < 2
    if by_pairs:
        places = [line, line ^ 1, jnp.where(low, 2, 1), jnp.where(low, 3, 0)]
    else:
        places = list(range(line_n))
    at = jnp.stack([side, inner, *places]).astype(jnp.int32)

    def keys_of(*stacked):
        if not by_pairs:
            sides = [[(k, place) for place in range(line_n)] for k in range(len(stacked))]
        else:
            sides = [
                [(3 * k, own), (3 * k + 1, of_next), (3 * k + 2, 0), (3 * k + 2, 1)]
                for k, (own, of_next) in enumerate(stacked)
            ]
        return sides[0] if len(sides) == 1 else list(zip(*sides, strict=True))

    def slots_of(*sides):
        return [ref for parts in sides for ref in (parts if by_pairs else parts[2:])]

    def ordered(own, got, axis):
        return jnp.where(
            side == 0, jnp.concatenate([own, got], axis), jnp.concatenate([got, own], axis)
        )

    def side_part(a, of):
        width = a.shape[-1] // side_n
        return lax.dynamic_slice_in_dim(a, of * width, width, a.ndim - 1)

    def everyone(a):
        return lax.all_gather(a, "mp", axis=0)

    def exchange(a):
        return lax.all_to_all(a, "dp", split_axis=0, concat_axis=0, tiled=True)

    positions = jnp.arange(span, dtype=jnp.int32)

    def live_of(lens):
        return (positions[None, :] < lens[:, None]).astype(jnp.int32).reshape(1, -1)


    fold = cross_kv.shape[1] // enc_out.shape[0]
    qkv_sent = jnp.concatenate([side_part(w, 1 - side) for w in enc_qkv], axis=1)
    qkv_sent, enc_out, val = fence(qkv_sent, enc_out, cross_kv[1])
    qkv_got = swap(qkv_sent)
    val = jnp.concatenate(jnp.split(val, fold, axis=0), axis=1)
    own_pair = jnp.stack([enc_out, val])
    qkv_own = jnp.concatenate([side_part(w, side) for w in enc_qkv], axis=1)
    pair_next = to_next(own_pair) if by_pairs else own_pair
    pair_inner = to_inner(own_pair) if by_pairs else own_pair
    tokens = take_rows(cand_embed, parent, 0).reshape(beam_n * span, local_width)
    lengths_got = swap(lengths)
    qkv_got, pair_next, pair_inner, tokens, lengths_got, qkv_own = fence(
        qkv_got, pair_next, pair_inner, tokens, lengths_got, qkv_own
    )

    both = jnp.zeros((side_n,) + qkv_own.shape, BF16)
    both = lax.dynamic_update_index_in_dim(both, qkv_own, side, 0)
    both = lax.dynamic_update_index_in_dim(both, qkv_got, 1 - side, 0)
    qkv_own = both.reshape(-1, both.shape[2])
    qkv_next = to_next(qkv_own) if by_pairs else qkv_own
    qkv_inner = to_inner(qkv_own) if by_pairs else qkv_own
    tokens_got = swap(tokens)
    own_blocks = everyone(tokens)
    source_rows = lax.all_gather(source[0], "mp", axis=1, tiled=True)
    source_cut = source_rows.reshape(query_n, dp_n, -1).transpose(1, 0, 2)
    source_cut = exchange(source_cut)
    cache = take_rows(kv_cache, parent, 1)
    owns = jnp.stack([enc_out, val, cross_out])
    qkv_next, qkv_inner, tokens_got, owns, pair_next, cache, source_cut = fence(
        qkv_next, qkv_inner, tokens_got, owns, pair_next, cache, source_cut
    )

    qkv_far = far(qkv_own, qkv_next, qkv_inner)
    got_blocks = everyone(tokens_got)
    owns_cross = swap(owns)
    pair_cross = swap(pair_next) if by_pairs else pair_next
    partial = exchange(dot(source_cut.reshape(dp_n * query_n, -1), cross_q))
    live = live_of(lengths)
    context = direct_context(
        live, hidden, wq_direct, wkv_direct, cache.reshape(2, beam_n * span, -1), span
    )
    context = lax.all_gather(context, "mp", axis=1, tiled=True)
    own_start = own_mp * local_width
    hidden_share = lax.dynamic_slice_in_dim(hidden, own_start, local_width, 1)
    new_state, *sums = direct_state(context, wo_direct, hidden_share, w_direct[None])
    squares, direct_dot = lax.psum(tuple(a.reshape(-1) for a in sums), "mp")
    direct_score = direct_dot / jnp.sqrt(squares / features + EPSILON)
    out_next, out_inner, val_next, val_inner = pair_next[0], pair_inner[0], pair_next[1], pair_inner[1]
    (
        qkv_far,
        owns_cross,
        pair_cross,
        (out_next, out_inner, val_next, val_inner),
        last_own,
        partial,
        new_state,
        direct_score,
        own_blocks,
        got_blocks,
    ) = fence(
        qkv_far,
        owns_cross,
        pair_cross,
        (out_next, out_inner, val_next, val_inner),
        cross_out,
        partial,
        new_state,
        direct_score,
        own_blocks,
        got_blocks,
    )

    out_far = far(enc_out, out_next, out_inner)
    last_next = to_next(last_own) if by_pairs else last_own
    if by_pairs:
        qkv_keys = [(0, None), (1, None), (2, None, 3), (4, None, 5)]
        outer, inner_last, outer_last = qkv_far
        qkv_slots = [qkv_own, qkv_next, qkv_inner, outer, inner_last, outer_last]
    else:
        qkv_keys, qkv_slots = keys_of((None, None)), qkv_far
    queries = jnp.sum(partial.reshape(dp_n, query_n, -1), axis=0).astype(BF16)
    queries = exchange(jnp.broadcast_to(queries, (dp_n,) + queries.shape).reshape(dp_n * query_n, -1))
    live_got = live_of(lengths_got)
    context_got = swap(enc_attention(at, got_blocks, live_got, qkv_keys, qkv_slots, span))
    context_own = enc_attention(at, own_blocks, live, qkv_keys, qkv_slots, span)
    enc_context = ordered(context_own, context_got, 1)
    enc_context, out_far, last_next, last_own, val_next, val_inner, queries = fence(
        enc_context, out_far, last_next, last_own, val_next, val_inner, queries
    )

    enc_blocks = everyone(enc_context)
    out_far = join(out_inner, out_far)
    out_cross = swap(out_far)
    val_far = far(val, val_next, val_inner)
    enc_blocks, out_cross, val_far, last_next, last_own, queries = fence(
        enc_blocks, out_cross, val_far, last_next, last_own, queries
    )
    summed, squares = encode_out(
        at,
        enc_blocks,
        tokens,
        keys_of((None, 0), (0, 0)),
        slots_of((enc_out, pair_next, out_far), (owns_cross, pair_cross, out_cross)),
    )
    memory_blocks = everyone(summed)
    val_far = join(val_inner, val_far)
    val_cross = swap(val_far)
    last_cross = swap(last_next) if by_pairs else last_next
    last_inner = to_inner(last_own) if by_pairs else last_own
    (last_inner,) = fence(last_inner)
    last_far = far(last_own, last_next, last_inner)
    head_n = queries.shape[1] // HD
    mixed = jnp.einsum(
        "rhc,khc->rhk",
        queries.reshape(-1, head_n, HD),
        cross_kv[0].reshape(-1, head_n, HD),
        preferred_element_type=F32,
    ).astype(BF16)
    depth = mixed.shape[2]
    pairs = head_n * query_n
    mixed = mixed.reshape(dp_n, query_n, head_n, depth).transpose(0, 2, 1, 3)
    mixed = exchange(mixed.reshape(dp_n, pairs, depth))
    mixed = mixed.reshape(line_n, side_n, pairs, depth).transpose(0, 2, 1, 3)
    mixed = mixed.reshape(line_n, pairs, side_n * depth)
    enc_squares = lax.psum(squares.reshape(1, -1), "mp").reshape(-1, 1)
    scale = 1.0 / jnp.sqrt(enc_squares / features + EPSILON)
    val_cross, last_cross, last_far = fence(val_cross, last_cross, last_far)
    last_far = join(last_inner, last_far)
    last_far_cross = swap(last_far)
    memory_blocks, scale, mixed = fence(memory_blocks, scale, mixed)

    cross_context = decode(
        at,
        memory_blocks,
        mixed,
        scale,
        live,
        keys_of((None, 1), (1, 1)),
        slots_of((val, pair_next, val_far), (owns_cross, pair_cross, val_cross)),
        span,
        query_n,
    )
    cross_blocks = everyone(cross_context)
    cross_blocks, last_far_cross = fence(cross_blocks, last_far_cross)
    dec_sums = decode_out(
        at,
        cross_blocks,
        source[0],
        w_channel[None],
        keys_of((None, None), (2, None)),
        slots_of((cross_out, last_next, last_far), (owns_cross, last_cross, last_far_cross)),
    )
    dec_squares, dec_dot = lax.psum(tuple(a.reshape(1, -1) for a in dec_sums), "mp")
    position_score = dec_dot / jnp.sqrt(dec_squares / features + EPSILON)
    own_channel = jnp.mean(position_score.reshape(beam_n, query_n), axis=1)
    shard_ids = lax.broadcasted_iota(jnp.int32, (dp_n, beam_n), 0)
    sent_scores = jnp.where(shard_ids == target_shard[None], own_channel[None], 0.0)
    return (new_state, direct_score + own_channel, jnp.sum(exchange(sent_scores), axis=0))


def solution(mesh):
    in_specs = (
        P("dp", None),
        P(None, "mp"),
        P(None, None, "mp"),
        P(None, "mp"),
        P(None, "dp", None, "mp"),
        P("dp"),
        P("dp"),
        P("dp", None, "mp"),
        P("dp", None, "mp"),
        P(None, "dp", "mp"),
        P("dp", "mp"),
        P("dp", "mp"),
        P(None, "dp", "mp"),
        P("dp", "mp"),
        P("mp"),
        P("mp"),
        P("dp"),
    )
    out_specs = (P("dp", "mp"), P("dp"), P("dp"))
    return jax.shard_map(shards, mesh=mesh, in_specs=in_specs, out_specs=out_specs, check_vma=False)
```

```python
import functools
import math

import jax
import jax.numpy as jnp
from jax import lax
from jax.experimental import pallas as pl
from jax.experimental.pallas import tpu as pltpu
from jax.sharding import PartitionSpec as P

HD = 64
EPSILON = 1e-06
NEG = -1e30
LANES = 128
F32 = jnp.float32
BF16 = jnp.bfloat16


def dot(a, b):
    return jnp.dot(a, b, preferred_element_type=F32)


def fence(*values):
    return lax.optimization_barrier(values)


def take_kernel(axis, index_ref, in_ref, out_ref):
    lead = (slice(None),) * axis
    for i in range(index_ref.shape[0]):
        out_ref[lead + (i,)] = in_ref[lead + (index_ref[i],)]


def take_rows(rows, index, axis):
    shape = rows.shape[:axis] + index.shape + rows.shape[axis + 1 :]
    return pl.pallas_call(
        functools.partial(take_kernel, axis),
        in_specs=[
            pl.BlockSpec(memory_space=pltpu.SMEM),
            pl.BlockSpec(memory_space=pltpu.VMEM),
        ],
        out_specs=pl.BlockSpec(memory_space=pltpu.VMEM),
        out_shape=jax.ShapeDtypeStruct(shape, rows.dtype),
        compiler_params=pltpu.CompilerParams(vmem_limit_bytes=16 << 20),
        cost_estimate=pl.CostEstimate(
            flops=0, bytes_accessed=4 * math.prod(shape), transcendentals=0
        ),
    )(index, rows)


VMEM = pl.BlockSpec(memory_space=pltpu.VMEM)
SMEM = pl.BlockSpec(memory_space=pltpu.SMEM)


def local_call(kernel, inputs, out_shapes, scratch=()):
    return pl.pallas_call(
        kernel,
        in_specs=[SMEM] + [VMEM] * (len(inputs) - 1),
        out_specs=[VMEM] * len(out_shapes),
        out_shape=[jax.ShapeDtypeStruct(*shape) for shape in out_shapes],
        scratch_shapes=[pltpu.VMEM(*shape) for shape in scratch],
        compiler_params=pltpu.CompilerParams(vmem_limit_bytes=36 << 20),
        cost_estimate=pl.CostEstimate(flops=1000, bytes_accessed=1000, transcendentals=0),
    )(*inputs)


def tile_of(n, most):
    return most if n % most == 0 else n


def for_tiles(n, body, most=256):
    tile = tile_of(n, most)
    if tile == n:
        body(pl.ds(0, n))
        return

    def step(i, carry):
        body(pl.ds(pl.multiple_of(i * tile, tile), tile))
        return carry

    lax.fori_loop(0, n // tile, step, 0)


def spread_tile(at_ref, blocks_ref, slots, rows, cols, fold_at=0):
    total = None
    for j, parts in enumerate(slots):
        place = at_ref[j + 2]
        for k, (ref, index, *other) in enumerate(parts):
            weights = load_part(ref, index, cols, fold_at)
            if other:
                weights = jnp.where(at_ref[1] == 1, weights, other[0][:, cols])
            lead = (place,) if len(parts) == 1 else (place, k)
            part = dot(blocks_ref[lead + (rows, slice(None))], weights)
            total = part if total is None else total + part
    return total


def load_part(ref, index, cols, fold_at):
    lead = () if index is None else (index,)
    part = ref[lead + (slice(None), cols)]
    if fold_at:
        right = pl.ds(cols.start + fold_at, cols.size)
        part = jnp.concatenate([part, ref[lead + (slice(None), right)]], axis=0)
    return part


def bind(keys, *refs):
    pairs = [key if isinstance(key[0], tuple) else (key,) for key in keys]
    return [[(refs[key[0]], key[1], *(refs[k] for k in key[2:])) for key in parts] for parts in pairs]


def enc_kernel(keys, slot_n, span, at_ref, blocks_ref, live_ref, *refs):
    slots = bind(keys, *refs[:slot_n])
    out_ref, qkv_ref = refs[slot_n:]
    total_rows, width = out_ref.shape

    def project(rows):
        def columns(cols):
            qkv_ref[rows, cols] = spread_tile(at_ref, blocks_ref, slots, rows, cols).astype(BF16)

        for_tiles(qkv_ref.shape[1], columns)

    for_tiles(total_rows, project, 512)
    own = lax.broadcasted_iota(jnp.int32, (LANES, LANES), 0) // span
    other = lax.broadcasted_iota(jnp.int32, (LANES, LANES), 1) // span
    same = own == other
    ones = jnp.ones((LANES, HD), BF16)
    for start in range(0, total_rows, LANES):
        rows = slice(start, start + LANES)
        bias = jnp.where(same & (live_ref[:, rows] > 0), 0.0, NEG)
        for head in range(width // HD):
            q, k, v = (
                qkv_ref[rows, part * width + head * HD : part * width + (head + 1) * HD]
                for part in range(3)
            )
            scores = lax.dot_general(q, k, (((1,), (1,)), ((), ())), preferred_element_type=F32)
            scores = scores * (1.0 / math.sqrt(HD)) + bias
            weights = jnp.exp(scores - jnp.max(scores, axis=1, keepdims=True)).astype(BF16)
            context = dot(weights, v) / dot(weights, ones)
            out_ref[rows, head * HD : (head + 1) * HD] = context.astype(BF16)


def enc_attention(at, blocks, live, keys, slots, span):
    rows, triple = blocks.shape[1], slots[0].shape[-1]
    return local_call(
        functools.partial(enc_kernel, keys, len(slots), span),
        (at, blocks, live, *slots),
        [((rows, triple // 3), BF16)],
        [((rows, triple), BF16)],
    )[0]


def out_kernel(keys, slot_n, at_ref, blocks_ref, tokens_ref, *refs):
    slots = bind(keys, *refs[:slot_n])
    summed_ref, squares_ref = refs[slot_n:]
    squares_ref[...] = jnp.zeros_like(squares_ref)

    side_n, total_rows, width = summed_ref.shape

    def row_tile(rows):
        for half in range(side_n):
            order = jnp.where(at_ref[0] == half, 0, 1)

            def columns(cols):
                start = cols.start + half * width
                if not isinstance(start, int):
                    start = pl.multiple_of(start, LANES)
                here = pl.ds(start, cols.size)
                summed = spread_tile(at_ref, blocks_ref, slots, rows, here)
                summed = summed + tokens_ref[rows, here].astype(F32)
                summed_ref[order, rows, cols] = summed.astype(BF16)
                squares_ref[rows] += jnp.sum(summed * summed, axis=1, keepdims=True)

            for_tiles(width, columns)

    for_tiles(total_rows, row_tile, 512)


def encode_out(at, blocks, tokens, keys, slots):
    return local_call(
        functools.partial(out_kernel, keys, len(slots)),
        (at, blocks, tokens, *slots),
        [((2, tokens.shape[0], tokens.shape[1] // 2), BF16), ((tokens.shape[0], 1), F32)],
    )


def decode_kernel(keys, slot_n, span, query_n, at_ref, blocks_ref, mixed_ref, column_ref, row_ref, live_ref, *refs):
    slots = bind(keys, *refs[:slot_n])
    out_ref, values_ref, scores_ref = refs[slot_n:]
    total_rows, width = values_ref.shape

    def project(rows):
        def columns(cols):
            values = spread_tile(at_ref, blocks_ref, slots, rows, cols, width) * column_ref[rows]
            values_ref[rows, cols] = values.astype(BF16)

        for_tiles(width, columns)

    for_tiles(total_rows, project, 512)
    total = None
    for k in range(blocks_ref.shape[0]):
        for half in range(blocks_ref.shape[1]):
            part = lax.dot_general(
                mixed_ref[k, jnp.where(at_ref[0] == 0, half, blocks_ref.shape[1] - 1 - half)],
                blocks_ref[k, half],
                (((1,), (1,)), ((), ())),
                preferred_element_type=F32,
            )
            total = part if total is None else total + part
    scores_ref[...] = total * (row_ref[...] * (1.0 / math.sqrt(HD)))
    pairs = scores_ref.shape[0]
    cands = LANES // span
    heads = pairs // query_n
    cand = lax.broadcasted_iota(jnp.int32, (pairs, LANES), 1) // span
    head = lax.broadcasted_iota(jnp.int32, (query_n, width), 1) // HD
    for at in range(total_rows // LANES):
        rows = slice(at * LANES, (at + 1) * LANES)
        scores = scores_ref[:, rows]
        live = live_ref[:, rows] > 0
        scores = jnp.concatenate(
            [jnp.where((cand == c) & live, scores, NEG) for c in range(cands)], axis=0
        )
        weights = jnp.exp(scores - jnp.max(scores, axis=1, keepdims=True))
        weights = (weights / jnp.sum(weights, axis=1, keepdims=True)).astype(BF16)
        context = dot(weights, values_ref[rows])
        made = []
        for c in range(cands):
            chosen = jnp.zeros((query_n, width), F32)
            for h in range(heads):
                start = (c * heads + h) * query_n
                chosen = chosen + jnp.where(head == h, context[start : start + query_n], 0.0)
            made.append(chosen)
        made = jnp.concatenate(made, axis=0).astype(BF16)
        half_width = width // 2
        for half in range(2):
            order = jnp.where(at_ref[0] == half, 0, 1)
            made_half = made[:, half * half_width : (half + 1) * half_width]
            out_ref[order, at * cands * query_n : (at + 1) * cands * query_n] = made_half


def decode(at, blocks, mixed, scale, live, keys, slots, span, query_n):
    rows, width = blocks.shape[2], slots[0].shape[-1] // 2
    return local_call(
        functools.partial(decode_kernel, keys, len(slots), span, query_n),
        (at, blocks, mixed, scale, scale.reshape(1, -1), live, *slots),
        [((2, rows // span * query_n, width // 2), BF16)],
        [((rows, width), BF16), ((mixed.shape[2], rows), F32)],
    )[0]


def last_kernel(keys, slot_n, at_ref, blocks_ref, source_ref, weight_ref, *refs):
    slots = bind(keys, *refs[:slot_n])
    squares_ref, dots_ref = refs[slot_n:]
    squares_ref[...] = jnp.zeros_like(squares_ref)
    dots_ref[...] = jnp.zeros_like(dots_ref)
    total_rows, query_n = squares_ref.shape[0], source_ref.shape[0]

    def columns(cols):
        update = spread_tile(at_ref, blocks_ref, slots, pl.ds(0, total_rows), cols)
        source = source_ref[:, cols].astype(F32)
        decoded = update + jnp.concatenate([source] * (total_rows // query_n), axis=0)
        squares_ref[...] += jnp.sum(decoded * decoded, axis=1, keepdims=True)
        weighted = decoded * weight_ref[:, cols].astype(F32)
        dots_ref[...] += jnp.sum(weighted, axis=1, keepdims=True)

    for_tiles(source_ref.shape[1], columns)


def decode_out(at, blocks, source, weight, keys, slots):
    column = ((blocks.shape[2], 1), F32)
    return local_call(
        functools.partial(last_kernel, keys, len(slots)),
        (at, blocks, source, weight, *slots),
        [column, column],
    )


def direct_kernel(span, live_ref, hidden_ref, wq_ref, wkv_ref, cache_ref, out_ref):
    beams, width = out_ref.shape
    heads = width // HD
    hidden = hidden_ref[...]
    query, key, value = (
        dot(hidden, weights).astype(BF16) for weights in (wq_ref[...], wkv_ref[0], wkv_ref[1])
    )
    column_head = lax.broadcasted_iota(jnp.int32, (beams, width), 1) // HD
    spread = jnp.concatenate(
        [jnp.where(column_head == h, query.astype(F32), 0.0) for h in range(heads)], axis=0
    ).astype(BF16)
    rows = heads * beams

    def product(keys):
        return lax.dot_general(spread, keys, (((1,), (1,)), ((), ())), preferred_element_type=F32)

    def beam_of(shape, axis, n):
        index = lax.broadcasted_iota(jnp.int32, shape, axis)
        return index % beams if axis == 0 else index // n

    old = (rows, beams * span)
    valid = (beam_of(old, 0, 1) == beam_of(old, 1, span)) & (live_ref[...] > 0)
    scores = jnp.where(valid, product(cache_ref[0]) * (1.0 / math.sqrt(HD)), NEG)
    new = (rows, beams)
    fresh = beam_of(new, 0, 1) == beam_of(new, 1, 1)
    scores_new = jnp.where(fresh, product(key) * (1.0 / math.sqrt(HD)), NEG)
    top = jnp.maximum(
        jnp.max(scores, axis=1, keepdims=True), jnp.max(scores_new, axis=1, keepdims=True)
    )
    weights, weights_new = jnp.exp(scores - top), jnp.exp(scores_new - top)
    total = jnp.sum(weights, axis=1, keepdims=True) + jnp.sum(weights_new, axis=1, keepdims=True)
    context = dot((weights / total).astype(BF16), cache_ref[1])
    context = context + dot((weights_new / total).astype(BF16), value)
    chosen = jnp.zeros((beams, width), F32)
    for h in range(heads):
        chosen = chosen + jnp.where(column_head == h, context[h * beams : (h + 1) * beams], 0.0)
    out_ref[...] = chosen.astype(BF16)


def direct_context(live, hidden, wq, wkv, cache, span):
    return pl.pallas_call(
        functools.partial(direct_kernel, span),
        in_specs=[VMEM] * 5,
        out_specs=VMEM,
        out_shape=jax.ShapeDtypeStruct((hidden.shape[0], wq.shape[1]), BF16),
        compiler_params=pltpu.CompilerParams(vmem_limit_bytes=36 << 20),
        cost_estimate=pl.CostEstimate(flops=1000, bytes_accessed=1000, transcendentals=0),
    )(live, hidden, wq, wkv, cache)


def state_kernel(context_ref, wo_ref, hidden_ref, weight_ref, state_ref, squares_ref, dots_ref):
    state = hidden_ref[...].astype(F32) + dot(context_ref[...], wo_ref[...])
    state_ref[...] = state.astype(BF16)
    squares_ref[...] = jnp.sum(state * state, axis=1, keepdims=True)
    dots_ref[...] = jnp.sum(state * weight_ref[...].astype(F32), axis=1, keepdims=True)


def direct_state(context, wo, hidden, weight):
    column = jax.ShapeDtypeStruct((hidden.shape[0], 1), F32)
    return pl.pallas_call(
        state_kernel,
        in_specs=[VMEM] * 4,
        out_specs=[VMEM] * 3,
        out_shape=[jax.ShapeDtypeStruct(hidden.shape, BF16), column, column],
        compiler_params=pltpu.CompilerParams(vmem_limit_bytes=36 << 20),
        cost_estimate=pl.CostEstimate(flops=1000, bytes_accessed=1000, transcendentals=0),
    )(context, wo, hidden, weight)


def shards(
    hidden,
    wq_direct,
    wkv_direct,
    wo_direct,
    kv_cache,
    parent,
    lengths,
    cand_embed,
    source,
    enc_qkv,
    enc_out,
    cross_q,
    cross_kv,
    cross_out,
    w_direct,
    w_channel,
    target_shard,
):
    dp_n, mp_n = lax.axis_size("dp"), lax.axis_size("mp")
    side_n = dp_n // mp_n
    line_n = dp_n // side_n
    me, own_mp = lax.axis_index("dp"), lax.axis_index("mp")
    side, line = me % side_n, me // side_n
    beam_n, features = hidden.shape
    span, query_n = kv_cache.shape[2], source.shape[1]
    local_width = cand_embed.shape[2]
    by_pairs = line_n == 4
    inner = (line == 1) | (line == 2)

    def move(a, pairs):
        return lax.ppermute(
            a, "dp", [(s * side_n + i, t * side_n + i) for s, t in pairs for i in range(side_n)]
        )

    def swap(a):
        return lax.ppermute(
            a, "dp", [(i, i - i % side_n + (i + 1) % side_n) for i in range(dp_n)]
        )

    def to_next(a):
        return move(a, [(0, 1), (1, 0), (2, 3), (3, 2)])

    def to_inner(a):
        return move(a, [(1, 2), (2, 1)])

    def far(own, of_next, of_inner):
        if not by_pairs:
            lines = [[k * side_n + i for k in range(line_n)] for i in range(side_n)]
            return [lax.all_gather(own, "dp", axis_index_groups=lines)]
        return [
            move(of_inner, [(1, 0), (2, 3)]),
            move(of_next, [(1, 2), (2, 1)]),
            move(of_next, [(1, 3), (2, 0)]),
        ]

    def join(of_inner, made):
        if not by_pairs:
            return made[0]
        outer, inner_last, outer_last = made
        return jnp.stack(
            [jnp.where(inner, of_inner, outer), jnp.where(inner, inner_last, outer_last)]
        )

    low = line < 2
    if by_pairs:
        places = [line, line ^ 1, jnp.where(low, 2, 1), jnp.where(low, 3, 0)]
    else:
        places = list(range(line_n))
    at = jnp.stack([side, inner, *places]).astype(jnp.int32)

    def keys_of(*stacked):
        if not by_pairs:
            sides = [[(k, place) for place in range(line_n)] for k in range(len(stacked))]
        else:
            sides = [
                [(3 * k, own), (3 * k + 1, of_next), (3 * k + 2, 0), (3 * k + 2, 1)]
                for k, (own, of_next) in enumerate(stacked)
            ]
        return sides[0] if len(sides) == 1 else list(zip(*sides, strict=True))

    def slots_of(*sides):
        return [ref for parts in sides for ref in (parts if by_pairs else parts[2:])]

    def side_part(a, of):
        width = a.shape[-1] // side_n
        return lax.dynamic_slice_in_dim(a, of * width, width, a.ndim - 1)

    def everyone(a):
        return lax.all_gather(a, "mp", axis=0)

    def exchange(a):
        return lax.all_to_all(a, "dp", split_axis=0, concat_axis=0, tiled=True)

    positions = jnp.arange(span, dtype=jnp.int32)

    def live_of(lens):
        return (positions[None, :] < lens[:, None]).astype(jnp.int32).reshape(1, -1)


    fold = cross_kv.shape[1] // enc_out.shape[0]
    qkv_sent = jnp.concatenate([side_part(w, 1 - side) for w in enc_qkv], axis=1)
    qkv_sent, enc_out, val = fence(qkv_sent, enc_out, cross_kv[1])
    qkv_got = swap(qkv_sent)
    val = jnp.concatenate(jnp.split(val, fold, axis=0), axis=1)
    own_pair = jnp.stack([enc_out, val])
    qkv_own = jnp.concatenate([side_part(w, side) for w in enc_qkv], axis=1)
    pair_next = to_next(own_pair) if by_pairs else own_pair
    pair_inner = to_inner(own_pair) if by_pairs else own_pair
    tokens = take_rows(cand_embed, parent, 0).reshape(beam_n * span, local_width)
    lengths_got = swap(lengths)
    qkv_got, pair_next, pair_inner, tokens, lengths_got, qkv_own = fence(
        qkv_got, pair_next, pair_inner, tokens, lengths_got, qkv_own
    )

    both = jnp.zeros((side_n,) + qkv_own.shape, BF16)
    both = lax.dynamic_update_index_in_dim(both, qkv_own, side, 0)
    both = lax.dynamic_update_index_in_dim(both, qkv_got, 1 - side, 0)
    qkv_own = both.reshape(-1, both.shape[2])
    qkv_next = to_next(qkv_own) if by_pairs else qkv_own
    qkv_inner = to_inner(qkv_own) if by_pairs else qkv_own
    tokens_got = swap(tokens)
    own_blocks = everyone(tokens)
    source_rows = lax.all_gather(source[0], "mp", axis=1, tiled=True)
    source_cut = source_rows.reshape(query_n, dp_n, -1).transpose(1, 0, 2)
    source_cut = exchange(source_cut)
    cache = take_rows(kv_cache, parent, 1)
    owns = jnp.stack([enc_out, val, cross_out])
    qkv_next, qkv_inner, tokens_got, owns, pair_next, cache, source_cut = fence(
        qkv_next, qkv_inner, tokens_got, owns, pair_next, cache, source_cut
    )

    qkv_far = far(qkv_own, qkv_next, qkv_inner)
    got_blocks = everyone(tokens_got)
    owns_cross = swap(owns)
    pair_cross = swap(pair_next) if by_pairs else pair_next
    partial = exchange(dot(source_cut.reshape(dp_n * query_n, -1), cross_q))
    live = live_of(lengths)
    context = direct_context(
        live, hidden, wq_direct, wkv_direct, cache.reshape(2, beam_n * span, -1), span
    )
    context = lax.all_gather(context, "mp", axis=1, tiled=True)
    own_start = own_mp * local_width
    hidden_share = lax.dynamic_slice_in_dim(hidden, own_start, local_width, 1)
    new_state, *sums = direct_state(context, wo_direct, hidden_share, w_direct[None])
    squares, direct_dot = lax.psum(tuple(a.reshape(-1) for a in sums), "mp")
    direct_score = direct_dot / jnp.sqrt(squares / features + EPSILON)
    out_next, out_inner, val_next, val_inner = pair_next[0], pair_inner[0], pair_next[1], pair_inner[1]
    (
        qkv_far,
        owns_cross,
        pair_cross,
        (out_next, out_inner, val_next, val_inner),
        last_own,
        partial,
        new_state,
        direct_score,
    ) = fence(
        qkv_far,
        owns_cross,
        pair_cross,
        (out_next, out_inner, val_next, val_inner),
        cross_out,
        partial,
        new_state,
        direct_score,
    )

    out_far = far(enc_out, out_next, out_inner)
    if by_pairs:
        qkv_keys = [(0, None), (1, None), (2, None, 3), (4, None, 5)]
        outer, inner_last, outer_last = qkv_far
        qkv_slots = [qkv_own, qkv_next, qkv_inner, outer, inner_last, outer_last]
    else:
        qkv_keys, qkv_slots = keys_of((None, None)), qkv_far
    live_got = live_of(lengths_got)
    context_got = swap(enc_attention(at, got_blocks, live_got, qkv_keys, qkv_slots, span))
    context_own = enc_attention(at, own_blocks, live, qkv_keys, qkv_slots, span)
    enc_context = jnp.stack([context_own, context_got])
    enc_context, out_far, last_own, val_next, val_inner, partial = fence(
        enc_context, out_far, last_own, val_next, val_inner, partial
    )

    enc_blocks = everyone(enc_context)
    out_far = join(out_inner, out_far)
    out_cross = swap(out_far)
    val_far = far(val, val_next, val_inner)
    queries = jnp.sum(partial.reshape(dp_n, query_n, -1), axis=0).astype(BF16)
    queries = exchange(jnp.broadcast_to(queries, (dp_n,) + queries.shape).reshape(dp_n * query_n, -1))
    enc_blocks, out_cross, val_far, last_own, queries = fence(
        enc_blocks, out_cross, val_far, last_own, queries
    )
    summed, squares = encode_out(
        at,
        enc_blocks,
        tokens,
        keys_of((None, 0), (0, 0)),
        slots_of((enc_out, pair_next, out_far), (owns_cross, pair_cross, out_cross)),
    )
    memory_blocks = everyone(summed)
    val_far = join(val_inner, val_far)
    val_cross = swap(val_far)
    last_next = to_next(last_own) if by_pairs else last_own
    last_inner = to_inner(last_own) if by_pairs else last_own
    last_next, last_inner = fence(last_next, last_inner)
    last_cross = swap(last_next) if by_pairs else last_next
    last_far = far(last_own, last_next, last_inner)
    head_n = queries.shape[1] // HD
    mixed = jnp.einsum(
        "rhc,khc->rhk",
        queries.reshape(-1, head_n, HD),
        cross_kv[0].reshape(-1, head_n, HD),
        preferred_element_type=F32,
    ).astype(BF16)
    depth = mixed.shape[2]
    pairs = head_n * query_n
    mixed = mixed.reshape(dp_n, query_n, head_n, depth).transpose(0, 2, 1, 3)
    mixed = exchange(mixed.reshape(dp_n, pairs, depth))
    mixed = mixed.reshape(line_n, side_n, pairs, depth)
    enc_squares = lax.psum(squares.reshape(1, -1), "mp").reshape(-1, 1)
    scale = 1.0 / jnp.sqrt(enc_squares / features + EPSILON)
    val_cross, last_cross, last_far, scale = fence(val_cross, last_cross, last_far, scale)
    last_far = join(last_inner, last_far)
    last_far_cross = swap(last_far)
    memory_blocks, mixed = fence(memory_blocks, mixed)

    cross_context = decode(
        at,
        memory_blocks,
        mixed,
        scale,
        live,
        keys_of((None, 1), (1, 1)),
        slots_of((val, pair_next, val_far), (owns_cross, pair_cross, val_cross)),
        span,
        query_n,
    )
    cross_blocks = everyone(cross_context)
    cross_blocks, last_far_cross = fence(cross_blocks, last_far_cross)
    dec_sums = decode_out(
        at,
        cross_blocks,
        source[0],
        w_channel[None],
        keys_of((None, None), (2, None)),
        slots_of((cross_out, last_next, last_far), (owns_cross, last_cross, last_far_cross)),
    )
    dec_squares, dec_dot = lax.psum(tuple(a.reshape(1, -1) for a in dec_sums), "mp")
    position_score = dec_dot / jnp.sqrt(dec_squares / features + EPSILON)
    own_channel = jnp.mean(position_score.reshape(beam_n, query_n), axis=1)
    shard_ids = lax.broadcasted_iota(jnp.int32, (dp_n, beam_n), 0)
    sent_scores = jnp.where(shard_ids == target_shard[None], own_channel[None], 0.0)
    return (new_state, direct_score + own_channel, jnp.sum(exchange(sent_scores), axis=0))


def solution(mesh):
    in_specs = (
        P("dp", None),
        P(None, "mp"),
        P(None, None, "mp"),
        P(None, "mp"),
        P(None, "dp", None, "mp"),
        P("dp"),
        P("dp"),
        P("dp", None, "mp"),
        P("dp", None, "mp"),
        P(None, "dp", "mp"),
        P("dp", "mp"),
        P("dp", "mp"),
        P(None, "dp", "mp"),
        P("dp", "mp"),
        P("mp"),
        P("mp"),
        P("dp"),
    )
    out_specs = (P("dp", "mp"), P("dp"), P("dp"))
    return jax.shard_map(shards, mesh=mesh, in_specs=in_specs, out_specs=out_specs, check_vma=False)
```

```python
import functools
import math

import jax
import jax.numpy as jnp
from jax import lax
from jax.experimental import pallas as pl
from jax.experimental.pallas import tpu as pltpu
from jax.sharding import PartitionSpec as P

HD = 64
EPSILON = 1e-06
NEG = -1e30
LANES = 128
F32 = jnp.float32
BF16 = jnp.bfloat16


def dot(a, b):
    return jnp.dot(a, b, preferred_element_type=F32)


def fence(*values):
    return lax.optimization_barrier(values)


def take_kernel(axis, index_ref, in_ref, out_ref):
    lead = (slice(None),) * axis
    for i in range(index_ref.shape[0]):
        out_ref[lead + (i,)] = in_ref[lead + (index_ref[i],)]


def take_rows(rows, index, axis):
    shape = rows.shape[:axis] + index.shape + rows.shape[axis + 1 :]
    return pl.pallas_call(
        functools.partial(take_kernel, axis),
        in_specs=[
            pl.BlockSpec(memory_space=pltpu.SMEM),
            pl.BlockSpec(memory_space=pltpu.VMEM),
        ],
        out_specs=pl.BlockSpec(memory_space=pltpu.VMEM),
        out_shape=jax.ShapeDtypeStruct(shape, rows.dtype),
        compiler_params=pltpu.CompilerParams(vmem_limit_bytes=16 << 20),
        cost_estimate=pl.CostEstimate(
            flops=0, bytes_accessed=4 * math.prod(shape), transcendentals=0
        ),
    )(index, rows)


VMEM = pl.BlockSpec(memory_space=pltpu.VMEM)
SMEM = pl.BlockSpec(memory_space=pltpu.SMEM)


def local_call(kernel, inputs, out_shapes, scratch=()):
    return pl.pallas_call(
        kernel,
        in_specs=[SMEM] + [VMEM] * (len(inputs) - 1),
        out_specs=[VMEM] * len(out_shapes),
        out_shape=[jax.ShapeDtypeStruct(*shape) for shape in out_shapes],
        scratch_shapes=[pltpu.VMEM(*shape) for shape in scratch],
        compiler_params=pltpu.CompilerParams(vmem_limit_bytes=36 << 20),
        cost_estimate=pl.CostEstimate(flops=1000, bytes_accessed=1000, transcendentals=0),
    )(*inputs)


def tile_of(n, most):
    return most if n % most == 0 else n


def for_tiles(n, body, most=256):
    tile = tile_of(n, most)
    if tile == n:
        body(pl.ds(0, n))
        return

    def step(i, carry):
        body(pl.ds(pl.multiple_of(i * tile, tile), tile))
        return carry

    lax.fori_loop(0, n // tile, step, 0)


def spread_tile(at_ref, blocks_ref, slots, rows, cols, fold_at=0):
    total = None
    for j, parts in enumerate(slots):
        place = at_ref[j + 2]
        for k, (ref, index, *other) in enumerate(parts):
            weights = load_part(ref, index, cols, fold_at)
            if other:
                weights = jnp.where(at_ref[1] == 1, weights, other[0][:, cols])
            lead = (place,) if len(parts) == 1 else (place, k)
            part = dot(blocks_ref[lead + (rows, slice(None))], weights)
            total = part if total is None else total + part
    return total


def load_part(ref, index, cols, fold_at):
    lead = () if index is None else (index,)
    part = ref[lead + (slice(None), cols)]
    if fold_at:
        right = pl.ds(cols.start + fold_at, cols.size)
        part = jnp.concatenate([part, ref[lead + (slice(None), right)]], axis=0)
    return part


def bind(keys, *refs):
    pairs = [key if isinstance(key[0], tuple) else (key,) for key in keys]
    return [[(refs[key[0]], key[1], *(refs[k] for k in key[2:])) for key in parts] for parts in pairs]


def enc_kernel(keys, slot_n, span, at_ref, blocks_ref, live_ref, *refs):
    slots = bind(keys, *refs[:slot_n])
    out_ref, qkv_ref = refs[slot_n:]
    total_rows, width = out_ref.shape

    def project(rows):
        def columns(cols):
            qkv_ref[rows, cols] = spread_tile(at_ref, blocks_ref, slots, rows, cols).astype(BF16)

        for_tiles(qkv_ref.shape[1], columns)

    for_tiles(total_rows, project, 512)
    own = lax.broadcasted_iota(jnp.int32, (LANES, LANES), 0) // span
    other = lax.broadcasted_iota(jnp.int32, (LANES, LANES), 1) // span
    same = own == other
    ones = jnp.ones((LANES, HD), BF16)
    for start in range(0, total_rows, LANES):
        rows = slice(start, start + LANES)
        bias = jnp.where(same & (live_ref[:, rows] > 0), 0.0, NEG)
        for head in range(width // HD):
            q, k, v = (
                qkv_ref[rows, part * width + head * HD : part * width + (head + 1) * HD]
                for part in range(3)
            )
            scores = lax.dot_general(q, k, (((1,), (1,)), ((), ())), preferred_element_type=F32)
            scores = scores * (1.0 / math.sqrt(HD)) + bias
            weights = jnp.exp(scores - jnp.max(scores, axis=1, keepdims=True)).astype(BF16)
            context = dot(weights, v) / dot(weights, ones)
            out_ref[rows, head * HD : (head + 1) * HD] = context.astype(BF16)


def enc_attention(at, blocks, live, keys, slots, span):
    rows, triple = blocks.shape[1], slots[0].shape[-1]
    return local_call(
        functools.partial(enc_kernel, keys, len(slots), span),
        (at, blocks, live, *slots),
        [((rows, triple // 3), BF16)],
        [((rows, triple), BF16)],
    )[0]


def out_kernel(keys, slot_n, at_ref, blocks_ref, tokens_ref, *refs):
    slots = bind(keys, *refs[:slot_n])
    summed_ref, squares_ref = refs[slot_n:]
    squares_ref[...] = jnp.zeros_like(squares_ref)

    side_n, total_rows, width = summed_ref.shape

    def row_tile(rows):
        for half in range(side_n):
            order = jnp.where(at_ref[0] == half, 0, 1)

            def columns(cols):
                start = cols.start + half * width
                if not isinstance(start, int):
                    start = pl.multiple_of(start, LANES)
                here = pl.ds(start, cols.size)
                summed = spread_tile(at_ref, blocks_ref, slots, rows, here)
                summed = summed + tokens_ref[rows, here].astype(F32)
                summed_ref[order, rows, cols] = summed.astype(BF16)
                squares_ref[rows] += jnp.sum(summed * summed, axis=1, keepdims=True)

            for_tiles(width, columns)

    for_tiles(total_rows, row_tile, 512)


def encode_out(at, blocks, tokens, keys, slots):
    return local_call(
        functools.partial(out_kernel, keys, len(slots)),
        (at, blocks, tokens, *slots),
        [((2, tokens.shape[0], tokens.shape[1] // 2), BF16), ((tokens.shape[0], 1), F32)],
    )


def decode_kernel(keys, slot_n, span, query_n, at_ref, blocks_ref, mixed_ref, column_ref, row_ref, live_ref, *refs):
    slots = bind(keys, *refs[:slot_n])
    out_ref, values_ref, scores_ref = refs[slot_n:]
    total_rows, width = values_ref.shape

    def project(rows):
        def columns(cols):
            values = spread_tile(at_ref, blocks_ref, slots, rows, cols, width) * column_ref[rows]
            values_ref[rows, cols] = values.astype(BF16)

        for_tiles(width, columns)

    for_tiles(total_rows, project, 512)
    total = None
    for k in range(blocks_ref.shape[0]):
        for half in range(blocks_ref.shape[1]):
            part = lax.dot_general(
                mixed_ref[k, jnp.where(at_ref[0] == 0, half, blocks_ref.shape[1] - 1 - half)],
                blocks_ref[k, half],
                (((1,), (1,)), ((), ())),
                preferred_element_type=F32,
            )
            total = part if total is None else total + part
    scores_ref[...] = total * (row_ref[...] * (1.0 / math.sqrt(HD)))
    pairs = scores_ref.shape[0]
    cands = LANES // span
    heads = pairs // query_n
    cand = lax.broadcasted_iota(jnp.int32, (pairs, LANES), 1) // span
    head = lax.broadcasted_iota(jnp.int32, (query_n, width), 1) // HD
    for at in range(total_rows // LANES):
        rows = slice(at * LANES, (at + 1) * LANES)
        scores = scores_ref[:, rows]
        live = live_ref[:, rows] > 0
        scores = jnp.concatenate(
            [jnp.where((cand == c) & live, scores, NEG) for c in range(cands)], axis=0
        )
        weights = jnp.exp(scores - jnp.max(scores, axis=1, keepdims=True))
        weights = (weights / jnp.sum(weights, axis=1, keepdims=True)).astype(BF16)
        context = dot(weights, values_ref[rows])
        made = []
        for c in range(cands):
            chosen = jnp.zeros((query_n, width), F32)
            for h in range(heads):
                start = (c * heads + h) * query_n
                chosen = chosen + jnp.where(head == h, context[start : start + query_n], 0.0)
            made.append(chosen)
        made = jnp.concatenate(made, axis=0).astype(BF16)
        half_width = width // 2
        for half in range(2):
            order = jnp.where(at_ref[0] == half, 0, 1)
            made_half = made[:, half * half_width : (half + 1) * half_width]
            out_ref[order, at * cands * query_n : (at + 1) * cands * query_n] = made_half


def decode(at, blocks, mixed, scale, live, keys, slots, span, query_n):
    rows, width = blocks.shape[2], slots[0].shape[-1] // 2
    return local_call(
        functools.partial(decode_kernel, keys, len(slots), span, query_n),
        (at, blocks, mixed, scale, scale.reshape(1, -1), live, *slots),
        [((2, rows // span * query_n, width // 2), BF16)],
        [((rows, width), BF16), ((mixed.shape[2], rows), F32)],
    )[0]


def last_kernel(keys, slot_n, at_ref, blocks_ref, source_ref, weight_ref, *refs):
    slots = bind(keys, *refs[:slot_n])
    squares_ref, dots_ref = refs[slot_n:]
    squares_ref[...] = jnp.zeros_like(squares_ref)
    dots_ref[...] = jnp.zeros_like(dots_ref)
    total_rows, query_n = squares_ref.shape[0], source_ref.shape[0]

    def columns(cols):
        update = spread_tile(at_ref, blocks_ref, slots, pl.ds(0, total_rows), cols)
        source = source_ref[:, cols].astype(F32)
        decoded = update + jnp.concatenate([source] * (total_rows // query_n), axis=0)
        squares_ref[...] += jnp.sum(decoded * decoded, axis=1, keepdims=True)
        weighted = decoded * weight_ref[:, cols].astype(F32)
        dots_ref[...] += jnp.sum(weighted, axis=1, keepdims=True)

    for_tiles(source_ref.shape[1], columns)


def decode_out(at, blocks, source, weight, keys, slots):
    column = ((blocks.shape[2], 1), F32)
    return local_call(
        functools.partial(last_kernel, keys, len(slots)),
        (at, blocks, source, weight, *slots),
        [column, column],
    )


def direct_kernel(span, live_ref, hidden_ref, wq_ref, wkv_ref, cache_ref, out_ref):
    beams, width = out_ref.shape
    heads = width // HD
    hidden = hidden_ref[...]
    query, key, value = (
        dot(hidden, weights).astype(BF16) for weights in (wq_ref[...], wkv_ref[0], wkv_ref[1])
    )
    column_head = lax.broadcasted_iota(jnp.int32, (beams, width), 1) // HD
    spread = jnp.concatenate(
        [jnp.where(column_head == h, query.astype(F32), 0.0) for h in range(heads)], axis=0
    ).astype(BF16)
    rows = heads * beams

    def product(keys):
        return lax.dot_general(spread, keys, (((1,), (1,)), ((), ())), preferred_element_type=F32)

    def beam_of(shape, axis, n):
        index = lax.broadcasted_iota(jnp.int32, shape, axis)
        return index % beams if axis == 0 else index // n

    old = (rows, beams * span)
    valid = (beam_of(old, 0, 1) == beam_of(old, 1, span)) & (live_ref[...] > 0)
    scores = jnp.where(valid, product(cache_ref[0]) * (1.0 / math.sqrt(HD)), NEG)
    new = (rows, beams)
    fresh = beam_of(new, 0, 1) == beam_of(new, 1, 1)
    scores_new = jnp.where(fresh, product(key) * (1.0 / math.sqrt(HD)), NEG)
    top = jnp.maximum(
        jnp.max(scores, axis=1, keepdims=True), jnp.max(scores_new, axis=1, keepdims=True)
    )
    weights, weights_new = jnp.exp(scores - top), jnp.exp(scores_new - top)
    total = jnp.sum(weights, axis=1, keepdims=True) + jnp.sum(weights_new, axis=1, keepdims=True)
    context = dot((weights / total).astype(BF16), cache_ref[1])
    context = context + dot((weights_new / total).astype(BF16), value)
    chosen = jnp.zeros((beams, width), F32)
    for h in range(heads):
        chosen = chosen + jnp.where(column_head == h, context[h * beams : (h + 1) * beams], 0.0)
    out_ref[...] = chosen.astype(BF16)


def direct_context(live, hidden, wq, wkv, cache, span):
    return pl.pallas_call(
        functools.partial(direct_kernel, span),
        in_specs=[VMEM] * 5,
        out_specs=VMEM,
        out_shape=jax.ShapeDtypeStruct((hidden.shape[0], wq.shape[1]), BF16),
        compiler_params=pltpu.CompilerParams(vmem_limit_bytes=36 << 20),
        cost_estimate=pl.CostEstimate(flops=1000, bytes_accessed=1000, transcendentals=0),
    )(live, hidden, wq, wkv, cache)


def state_kernel(context_ref, wo_ref, hidden_ref, weight_ref, state_ref, squares_ref, dots_ref):
    state = hidden_ref[...].astype(F32) + dot(context_ref[...], wo_ref[...])
    state_ref[...] = state.astype(BF16)
    squares_ref[...] = jnp.sum(state * state, axis=1, keepdims=True)
    dots_ref[...] = jnp.sum(state * weight_ref[...].astype(F32), axis=1, keepdims=True)


def direct_state(context, wo, hidden, weight):
    column = jax.ShapeDtypeStruct((hidden.shape[0], 1), F32)
    return pl.pallas_call(
        state_kernel,
        in_specs=[VMEM] * 4,
        out_specs=[VMEM] * 3,
        out_shape=[jax.ShapeDtypeStruct(hidden.shape, BF16), column, column],
        compiler_params=pltpu.CompilerParams(vmem_limit_bytes=36 << 20),
        cost_estimate=pl.CostEstimate(flops=1000, bytes_accessed=1000, transcendentals=0),
    )(context, wo, hidden, weight)


def shards(
    hidden,
    wq_direct,
    wkv_direct,
    wo_direct,
    kv_cache,
    parent,
    lengths,
    cand_embed,
    source,
    enc_qkv,
    enc_out,
    cross_q,
    cross_kv,
    cross_out,
    w_direct,
    w_channel,
    target_shard,
):
    dp_n, mp_n = lax.axis_size("dp"), lax.axis_size("mp")
    side_n = dp_n // mp_n
    line_n = dp_n // side_n
    me, own_mp = lax.axis_index("dp"), lax.axis_index("mp")
    side, line = me % side_n, me // side_n
    beam_n, features = hidden.shape
    span, query_n = kv_cache.shape[2], source.shape[1]
    local_width = cand_embed.shape[2]
    by_pairs = line_n == 4
    inner = (line == 1) | (line == 2)

    def move(a, pairs):
        return lax.ppermute(
            a, "dp", [(s * side_n + i, t * side_n + i) for s, t in pairs for i in range(side_n)]
        )

    def swap(a):
        return lax.ppermute(
            a, "dp", [(i, i - i % side_n + (i + 1) % side_n) for i in range(dp_n)]
        )

    def to_next(a):
        return move(a, [(0, 1), (1, 0), (2, 3), (3, 2)])

    def to_inner(a):
        return move(a, [(1, 2), (2, 1)])

    def far(own, of_next, of_inner):
        if not by_pairs:
            lines = [[k * side_n + i for k in range(line_n)] for i in range(side_n)]
            return [lax.all_gather(own, "dp", axis_index_groups=lines)]
        return [
            move(of_inner, [(1, 0), (2, 3)]),
            move(of_next, [(1, 2), (2, 1)]),
            move(of_next, [(1, 3), (2, 0)]),
        ]

    def join(of_inner, made):
        if not by_pairs:
            return made[0]
        outer, inner_last, outer_last = made
        return jnp.stack(
            [jnp.where(inner, of_inner, outer), jnp.where(inner, inner_last, outer_last)]
        )

    low = line < 2
    if by_pairs:
        places = [line, line ^ 1, jnp.where(low, 2, 1), jnp.where(low, 3, 0)]
    else:
        places = list(range(line_n))
    at = jnp.stack([side, inner, *places]).astype(jnp.int32)

    def keys_of(*stacked):
        if not by_pairs:
            sides = [[(k, place) for place in range(line_n)] for k in range(len(stacked))]
        else:
            sides = [
                [(3 * k, own), (3 * k + 1, of_next), (3 * k + 2, 0), (3 * k + 2, 1)]
                for k, (own, of_next) in enumerate(stacked)
            ]
        return sides[0] if len(sides) == 1 else list(zip(*sides, strict=True))

    def slots_of(*sides):
        return [ref for parts in sides for ref in (parts if by_pairs else parts[2:])]

    def side_part(a, of):
        width = a.shape[-1] // side_n
        return lax.dynamic_slice_in_dim(a, of * width, width, a.ndim - 1)

    def everyone(a):
        return lax.all_gather(a, "mp", axis=0)

    def exchange(a):
        return lax.all_to_all(a, "dp", split_axis=0, concat_axis=0, tiled=True)

    positions = jnp.arange(span, dtype=jnp.int32)

    def live_of(lens):
        return (positions[None, :] < lens[:, None]).astype(jnp.int32).reshape(1, -1)


    fold = cross_kv.shape[1] // enc_out.shape[0]
    qkv_sent = jnp.concatenate([side_part(w, 1 - side) for w in enc_qkv], axis=1)
    qkv_sent, enc_out, val = fence(qkv_sent, enc_out, cross_kv[1])
    qkv_got = swap(qkv_sent)
    val = jnp.concatenate(jnp.split(val, fold, axis=0), axis=1)
    qkv_own = jnp.concatenate([side_part(w, side) for w in enc_qkv], axis=1)
    out_next, val_next = (to_next(a) if by_pairs else a for a in (enc_out, val))
    out_inner, val_inner = (to_inner(a) if by_pairs else a for a in (enc_out, val))
    tokens = take_rows(cand_embed, parent, 0).reshape(beam_n * span, local_width)
    qkv_got, out_next, val_next, out_inner, val_inner, tokens, qkv_own = fence(
        qkv_got, out_next, val_next, out_inner, val_inner, tokens, qkv_own
    )

    both = jnp.zeros((side_n,) + qkv_own.shape, BF16)
    both = lax.dynamic_update_index_in_dim(both, qkv_own, side, 0)
    both = lax.dynamic_update_index_in_dim(both, qkv_got, 1 - side, 0)
    qkv_own = both.reshape(-1, both.shape[2])
    qkv_next = to_next(qkv_own) if by_pairs else qkv_own
    qkv_inner = to_inner(qkv_own) if by_pairs else qkv_own
    tokens_got = swap(tokens)
    lengths_got = swap(lengths)
    pair_next = jnp.stack([out_next, val_next])
    own_blocks = everyone(tokens)
    source_rows = lax.all_gather(source[0], "mp", axis=1, tiled=True)
    source_cut = source_rows.reshape(query_n, dp_n, -1).transpose(1, 0, 2)
    source_cut = exchange(source_cut)
    cache = take_rows(kv_cache, parent, 1)
    owns = jnp.stack([enc_out, val, cross_out])
    qkv_next, qkv_inner, tokens_got, lengths_got, owns, pair_next, cache, source_cut = fence(
        qkv_next, qkv_inner, tokens_got, lengths_got, owns, pair_next, cache, source_cut
    )

    qkv_far = far(qkv_own, qkv_next, qkv_inner)
    got_blocks = everyone(tokens_got)
    owns_cross = swap(owns)
    pair_cross = swap(pair_next) if by_pairs else pair_next
    partial = exchange(dot(source_cut.reshape(dp_n * query_n, -1), cross_q))
    live = live_of(lengths)
    context = direct_context(
        live, hidden, wq_direct, wkv_direct, cache.reshape(2, beam_n * span, -1), span
    )
    context = lax.all_gather(context, "mp", axis=1, tiled=True)
    own_start = own_mp * local_width
    hidden_share = lax.dynamic_slice_in_dim(hidden, own_start, local_width, 1)
    new_state, *sums = direct_state(context, wo_direct, hidden_share, w_direct[None])
    squares, direct_dot = lax.psum(tuple(a.reshape(-1) for a in sums), "mp")
    direct_score = direct_dot / jnp.sqrt(squares / features + EPSILON)
    (
        qkv_far,
        owns_cross,
        pair_cross,
        (out_next, out_inner, val_next, val_inner),
        last_own,
        partial,
        new_state,
        direct_score,
    ) = fence(
        qkv_far,
        owns_cross,
        pair_cross,
        (out_next, out_inner, val_next, val_inner),
        cross_out,
        partial,
        new_state,
        direct_score,
    )

    out_far = far(enc_out, out_next, out_inner)
    if by_pairs:
        qkv_keys = [(0, None), (1, None), (2, None, 3), (4, None, 5)]
        outer, inner_last, outer_last = qkv_far
        qkv_slots = [qkv_own, qkv_next, qkv_inner, outer, inner_last, outer_last]
    else:
        qkv_keys, qkv_slots = keys_of((None, None)), qkv_far
    live_got = live_of(lengths_got)
    context_got = swap(enc_attention(at, got_blocks, live_got, qkv_keys, qkv_slots, span))
    context_own = enc_attention(at, own_blocks, live, qkv_keys, qkv_slots, span)
    enc_context = jnp.stack([context_own, context_got])
    enc_context, out_far, last_own, val_next, val_inner, partial = fence(
        enc_context, out_far, last_own, val_next, val_inner, partial
    )

    enc_blocks = everyone(enc_context)
    out_far = join(out_inner, out_far)
    out_cross = swap(out_far)
    val_far = far(val, val_next, val_inner)
    queries = jnp.sum(partial.reshape(dp_n, query_n, -1), axis=0).astype(BF16)
    queries = exchange(jnp.broadcast_to(queries, (dp_n,) + queries.shape).reshape(dp_n * query_n, -1))
    enc_blocks, out_cross, val_far, last_own, queries = fence(
        enc_blocks, out_cross, val_far, last_own, queries
    )
    summed, squares = encode_out(
        at,
        enc_blocks,
        tokens,
        keys_of((None, 0), (0, 0)),
        slots_of((enc_out, pair_next, out_far), (owns_cross, pair_cross, out_cross)),
    )
    memory_blocks = everyone(summed)
    val_far = join(val_inner, val_far)
    val_cross = swap(val_far)
    last_next = to_next(last_own) if by_pairs else last_own
    last_inner = to_inner(last_own) if by_pairs else last_own
    last_next, last_inner = fence(last_next, last_inner)
    last_cross = swap(last_next) if by_pairs else last_next
    last_far = far(last_own, last_next, last_inner)
    head_n = queries.shape[1] // HD
    mixed = jnp.einsum(
        "rhc,khc->rhk",
        queries.reshape(-1, head_n, HD),
        cross_kv[0].reshape(-1, head_n, HD),
        preferred_element_type=F32,
    ).astype(BF16)
    depth = mixed.shape[2]
    pairs = head_n * query_n
    mixed = mixed.reshape(dp_n, query_n, head_n, depth).transpose(0, 2, 1, 3)
    mixed = exchange(mixed.reshape(dp_n, pairs, depth))
    mixed = mixed.reshape(line_n, side_n, pairs, depth)
    enc_squares = lax.psum(squares.reshape(1, -1), "mp").reshape(-1, 1)
    scale = 1.0 / jnp.sqrt(enc_squares / features + EPSILON)
    val_cross, last_cross, last_far, scale = fence(val_cross, last_cross, last_far, scale)
    last_far = join(last_inner, last_far)
    last_far_cross = swap(last_far)
    memory_blocks, mixed = fence(memory_blocks, mixed)

    cross_context = decode(
        at,
        memory_blocks,
        mixed,
        scale,
        live,
        keys_of((None, 1), (1, 1)),
        slots_of((val, pair_next, val_far), (owns_cross, pair_cross, val_cross)),
        span,
        query_n,
    )
    cross_blocks = everyone(cross_context)
    cross_blocks, last_far_cross = fence(cross_blocks, last_far_cross)
    dec_sums = decode_out(
        at,
        cross_blocks,
        source[0],
        w_channel[None],
        keys_of((None, None), (2, None)),
        slots_of((cross_out, last_next, last_far), (owns_cross, last_cross, last_far_cross)),
    )
    dec_squares, dec_dot = lax.psum(tuple(a.reshape(1, -1) for a in dec_sums), "mp")
    position_score = dec_dot / jnp.sqrt(dec_squares / features + EPSILON)
    own_channel = jnp.mean(position_score.reshape(beam_n, query_n), axis=1)
    shard_ids = lax.broadcasted_iota(jnp.int32, (dp_n, beam_n), 0)
    sent_scores = jnp.where(shard_ids == target_shard[None], own_channel[None], 0.0)
    return (new_state, direct_score + own_channel, jnp.sum(exchange(sent_scores), axis=0))


def solution(mesh):
    in_specs = (
        P("dp", None),
        P(None, "mp"),
        P(None, None, "mp"),
        P(None, "mp"),
        P(None, "dp", None, "mp"),
        P("dp"),
        P("dp"),
        P("dp", None, "mp"),
        P("dp", None, "mp"),
        P(None, "dp", "mp"),
        P("dp", "mp"),
        P("dp", "mp"),
        P(None, "dp", "mp"),
        P("dp", "mp"),
        P("mp"),
        P("mp"),
        P("dp"),
    )
    out_specs = (P("dp", "mp"), P("dp"), P("dp"))
    return jax.shard_map(shards, mesh=mesh, in_specs=in_specs, out_specs=out_specs, check_vma=False)
```

```python
import functools
import math

import jax
import jax.numpy as jnp
from jax import lax
from jax.experimental import pallas as pl
from jax.experimental.pallas import tpu as pltpu
from jax.sharding import PartitionSpec as P

HD = 64
EPSILON = 1e-06
NEG = -1e30
LANES = 128
F32 = jnp.float32
BF16 = jnp.bfloat16


def dot(a, b):
    return jnp.dot(a, b, preferred_element_type=F32)


def fence(*values):
    return lax.optimization_barrier(values)


def take_kernel(axis, index_ref, in_ref, out_ref):
    lead = (slice(None),) * axis
    for i in range(index_ref.shape[0]):
        out_ref[lead + (i,)] = in_ref[lead + (index_ref[i],)]


def take_rows(rows, index, axis):
    shape = rows.shape[:axis] + index.shape + rows.shape[axis + 1 :]
    return pl.pallas_call(
        functools.partial(take_kernel, axis),
        in_specs=[
            pl.BlockSpec(memory_space=pltpu.SMEM),
            pl.BlockSpec(memory_space=pltpu.VMEM),
        ],
        out_specs=pl.BlockSpec(memory_space=pltpu.VMEM),
        out_shape=jax.ShapeDtypeStruct(shape, rows.dtype),
        compiler_params=pltpu.CompilerParams(vmem_limit_bytes=16 << 20),
        cost_estimate=pl.CostEstimate(
            flops=0, bytes_accessed=4 * math.prod(shape), transcendentals=0
        ),
    )(index, rows)


VMEM = pl.BlockSpec(memory_space=pltpu.VMEM)
SMEM = pl.BlockSpec(memory_space=pltpu.SMEM)


def local_call(kernel, inputs, out_shapes, scratch=()):
    return pl.pallas_call(
        kernel,
        in_specs=[SMEM] + [VMEM] * (len(inputs) - 1),
        out_specs=[VMEM] * len(out_shapes),
        out_shape=[jax.ShapeDtypeStruct(*shape) for shape in out_shapes],
        scratch_shapes=[pltpu.VMEM(*shape) for shape in scratch],
        compiler_params=pltpu.CompilerParams(vmem_limit_bytes=36 << 20),
        cost_estimate=pl.CostEstimate(flops=1000, bytes_accessed=1000, transcendentals=0),
    )(*inputs)


def tile_of(n, most):
    return most if n % most == 0 else n


def for_tiles(n, body, most=256):
    tile = tile_of(n, most)
    if tile == n:
        body(pl.ds(0, n))
        return

    def step(i, carry):
        body(pl.ds(pl.multiple_of(i * tile, tile), tile))
        return carry

    lax.fori_loop(0, n // tile, step, 0)


def spread_tile(at_ref, blocks_ref, slots, rows, cols, fold_at=0):
    total = None
    for j, parts in enumerate(slots):
        place = at_ref[j + 2]
        for k, (ref, index, *other) in enumerate(parts):
            weights = load_part(ref, index, cols, fold_at)
            if other:
                weights = jnp.where(at_ref[1] == 1, weights, other[0][:, cols])
            lead = (place,) if len(parts) == 1 else (place, k)
            part = dot(blocks_ref[lead + (rows, slice(None))], weights)
            total = part if total is None else total + part
    return total


def load_part(ref, index, cols, fold_at):
    lead = () if index is None else (index,)
    part = ref[lead + (slice(None), cols)]
    if fold_at:
        right = pl.ds(cols.start + fold_at, cols.size)
        part = jnp.concatenate([part, ref[lead + (slice(None), right)]], axis=0)
    return part


def bind(keys, *refs):
    pairs = [key if isinstance(key[0], tuple) else (key,) for key in keys]
    return [[(refs[key[0]], key[1], *(refs[k] for k in key[2:])) for key in parts] for parts in pairs]


def enc_kernel(keys, slot_n, span, at_ref, blocks_ref, live_ref, *refs):
    slots = bind(keys, *refs[:slot_n])
    out_ref, qkv_ref = refs[slot_n:]
    total_rows, width = out_ref.shape

    def project(rows):
        def columns(cols):
            qkv_ref[rows, cols] = spread_tile(at_ref, blocks_ref, slots, rows, cols).astype(BF16)

        for_tiles(qkv_ref.shape[1], columns)

    for_tiles(total_rows, project, 512)
    own = lax.broadcasted_iota(jnp.int32, (LANES, LANES), 0) // span
    other = lax.broadcasted_iota(jnp.int32, (LANES, LANES), 1) // span
    same = own == other
    ones = jnp.ones((LANES, HD), BF16)
    for start in range(0, total_rows, LANES):
        rows = slice(start, start + LANES)
        bias = jnp.where(same & (live_ref[:, rows] > 0), 0.0, NEG)
        for head in range(width // HD):
            q, k, v = (
                qkv_ref[rows, part * width + head * HD : part * width + (head + 1) * HD]
                for part in range(3)
            )
            scores = lax.dot_general(q, k, (((1,), (1,)), ((), ())), preferred_element_type=F32)
            scores = scores * (1.0 / math.sqrt(HD)) + bias
            weights = jnp.exp(scores - jnp.max(scores, axis=1, keepdims=True)).astype(BF16)
            context = dot(weights, v) / dot(weights, ones)
            out_ref[rows, head * HD : (head + 1) * HD] = context.astype(BF16)


def enc_attention(at, blocks, live, keys, slots, span):
    rows, triple = blocks.shape[1], slots[0].shape[-1]
    return local_call(
        functools.partial(enc_kernel, keys, len(slots), span),
        (at, blocks, live, *slots),
        [((rows, triple // 3), BF16)],
        [((rows, triple), BF16)],
    )[0]


def out_kernel(keys, slot_n, at_ref, blocks_ref, tokens_ref, *refs):
    slots = bind(keys, *refs[:slot_n])
    summed_ref, squares_ref = refs[slot_n:]
    squares_ref[...] = jnp.zeros_like(squares_ref)

    side_n, total_rows, width = summed_ref.shape

    def row_tile(rows):
        for half in range(side_n):
            order = jnp.where(at_ref[0] == half, 0, 1)

            def columns(cols):
                start = cols.start + half * width
                if not isinstance(start, int):
                    start = pl.multiple_of(start, LANES)
                here = pl.ds(start, cols.size)
                summed = spread_tile(at_ref, blocks_ref, slots, rows, here)
                summed = summed + tokens_ref[rows, here].astype(F32)
                summed_ref[order, rows, cols] = summed.astype(BF16)
                squares_ref[rows] += jnp.sum(summed * summed, axis=1, keepdims=True)

            for_tiles(width, columns)

    for_tiles(total_rows, row_tile, 512)


def encode_out(at, blocks, tokens, keys, slots):
    return local_call(
        functools.partial(out_kernel, keys, len(slots)),
        (at, blocks, tokens, *slots),
        [((2, tokens.shape[0], tokens.shape[1] // 2), BF16), ((tokens.shape[0], 1), F32)],
    )


def decode_kernel(keys, slot_n, span, query_n, at_ref, blocks_ref, mixed_ref, column_ref, row_ref, live_ref, *refs):
    slots = bind(keys, *refs[:slot_n])
    out_ref, values_ref, scores_ref = refs[slot_n:]
    total_rows, width = values_ref.shape

    def project(rows):
        def columns(cols):
            values = spread_tile(at_ref, blocks_ref, slots, rows, cols, width) * column_ref[rows]
            values_ref[rows, cols] = values.astype(BF16)

        for_tiles(width, columns)

    for_tiles(total_rows, project, 512)
    total = None
    for k in range(blocks_ref.shape[0]):
        for half in range(blocks_ref.shape[1]):
            part = lax.dot_general(
                mixed_ref[k, jnp.where(at_ref[0] == 0, half, blocks_ref.shape[1] - 1 - half)],
                blocks_ref[k, half],
                (((1,), (1,)), ((), ())),
                preferred_element_type=F32,
            )
            total = part if total is None else total + part
    scores_ref[...] = total * (row_ref[...] * (1.0 / math.sqrt(HD)))
    pairs = scores_ref.shape[0]
    cands = LANES // span
    heads = pairs // query_n
    cand = lax.broadcasted_iota(jnp.int32, (pairs, LANES), 1) // span
    head = lax.broadcasted_iota(jnp.int32, (query_n, width), 1) // HD
    for at in range(total_rows // LANES):
        rows = slice(at * LANES, (at + 1) * LANES)
        scores = scores_ref[:, rows]
        live = live_ref[:, rows] > 0
        scores = jnp.concatenate(
            [jnp.where((cand == c) & live, scores, NEG) for c in range(cands)], axis=0
        )
        weights = jnp.exp(scores - jnp.max(scores, axis=1, keepdims=True))
        weights = (weights / jnp.sum(weights, axis=1, keepdims=True)).astype(BF16)
        context = dot(weights, values_ref[rows])
        made = []
        for c in range(cands):
            chosen = jnp.zeros((query_n, width), F32)
            for h in range(heads):
                start = (c * heads + h) * query_n
                chosen = chosen + jnp.where(head == h, context[start : start + query_n], 0.0)
            made.append(chosen)
        made = jnp.concatenate(made, axis=0).astype(BF16)
        half_width = width // 2
        for half in range(2):
            order = jnp.where(at_ref[0] == half, 0, 1)
            made_half = made[:, half * half_width : (half + 1) * half_width]
            out_ref[order, at * cands * query_n : (at + 1) * cands * query_n] = made_half


def decode(at, blocks, mixed, scale, live, keys, slots, span, query_n):
    rows, width = blocks.shape[2], slots[0].shape[-1] // 2
    return local_call(
        functools.partial(decode_kernel, keys, len(slots), span, query_n),
        (at, blocks, mixed, scale, scale.reshape(1, -1), live, *slots),
        [((2, rows // span * query_n, width // 2), BF16)],
        [((rows, width), BF16), ((mixed.shape[2], rows), F32)],
    )[0]


def last_kernel(keys, slot_n, at_ref, blocks_ref, source_ref, weight_ref, *refs):
    slots = bind(keys, *refs[:slot_n])
    squares_ref, dots_ref = refs[slot_n:]
    squares_ref[...] = jnp.zeros_like(squares_ref)
    dots_ref[...] = jnp.zeros_like(dots_ref)
    total_rows, query_n = squares_ref.shape[0], source_ref.shape[0]

    def columns(cols):
        update = spread_tile(at_ref, blocks_ref, slots, pl.ds(0, total_rows), cols)
        source = source_ref[:, cols].astype(F32)
        decoded = update + jnp.concatenate([source] * (total_rows // query_n), axis=0)
        squares_ref[...] += jnp.sum(decoded * decoded, axis=1, keepdims=True)
        weighted = decoded * weight_ref[:, cols].astype(F32)
        dots_ref[...] += jnp.sum(weighted, axis=1, keepdims=True)

    for_tiles(source_ref.shape[1], columns)


def decode_out(at, blocks, source, weight, keys, slots):
    column = ((blocks.shape[2], 1), F32)
    return local_call(
        functools.partial(last_kernel, keys, len(slots)),
        (at, blocks, source, weight, *slots),
        [column, column],
    )


def direct_kernel(span, live_ref, hidden_ref, wq_ref, wkv_ref, cache_ref, out_ref):
    beams, width = out_ref.shape
    heads = width // HD
    hidden = hidden_ref[...]
    query, key, value = (
        dot(hidden, weights).astype(BF16) for weights in (wq_ref[...], wkv_ref[0], wkv_ref[1])
    )
    column_head = lax.broadcasted_iota(jnp.int32, (beams, width), 1) // HD
    spread = jnp.concatenate(
        [jnp.where(column_head == h, query.astype(F32), 0.0) for h in range(heads)], axis=0
    ).astype(BF16)
    rows = heads * beams

    def product(keys):
        return lax.dot_general(spread, keys, (((1,), (1,)), ((), ())), preferred_element_type=F32)

    def beam_of(shape, axis, n):
        index = lax.broadcasted_iota(jnp.int32, shape, axis)
        return index % beams if axis == 0 else index // n

    old = (rows, beams * span)
    valid = (beam_of(old, 0, 1) == beam_of(old, 1, span)) & (live_ref[...] > 0)
    scores = jnp.where(valid, product(cache_ref[0]) * (1.0 / math.sqrt(HD)), NEG)
    new = (rows, beams)
    fresh = beam_of(new, 0, 1) == beam_of(new, 1, 1)
    scores_new = jnp.where(fresh, product(key) * (1.0 / math.sqrt(HD)), NEG)
    top = jnp.maximum(
        jnp.max(scores, axis=1, keepdims=True), jnp.max(scores_new, axis=1, keepdims=True)
    )
    weights, weights_new = jnp.exp(scores - top), jnp.exp(scores_new - top)
    total = jnp.sum(weights, axis=1, keepdims=True) + jnp.sum(weights_new, axis=1, keepdims=True)
    context = dot((weights / total).astype(BF16), cache_ref[1])
    context = context + dot((weights_new / total).astype(BF16), value)
    chosen = jnp.zeros((beams, width), F32)
    for h in range(heads):
        chosen = chosen + jnp.where(column_head == h, context[h * beams : (h + 1) * beams], 0.0)
    out_ref[...] = chosen.astype(BF16)


def direct_context(live, hidden, wq, wkv, cache, span):
    return pl.pallas_call(
        functools.partial(direct_kernel, span),
        in_specs=[VMEM] * 5,
        out_specs=VMEM,
        out_shape=jax.ShapeDtypeStruct((hidden.shape[0], wq.shape[1]), BF16),
        compiler_params=pltpu.CompilerParams(vmem_limit_bytes=36 << 20),
        cost_estimate=pl.CostEstimate(flops=1000, bytes_accessed=1000, transcendentals=0),
    )(live, hidden, wq, wkv, cache)


def state_kernel(context_ref, wo_ref, hidden_ref, weight_ref, state_ref, squares_ref, dots_ref):
    state = hidden_ref[...].astype(F32) + dot(context_ref[...], wo_ref[...])
    state_ref[...] = state.astype(BF16)
    squares_ref[...] = jnp.sum(state * state, axis=1, keepdims=True)
    dots_ref[...] = jnp.sum(state * weight_ref[...].astype(F32), axis=1, keepdims=True)


def direct_state(context, wo, hidden, weight):
    column = jax.ShapeDtypeStruct((hidden.shape[0], 1), F32)
    return pl.pallas_call(
        state_kernel,
        in_specs=[VMEM] * 4,
        out_specs=[VMEM] * 3,
        out_shape=[jax.ShapeDtypeStruct(hidden.shape, BF16), column, column],
        compiler_params=pltpu.CompilerParams(vmem_limit_bytes=36 << 20),
        cost_estimate=pl.CostEstimate(flops=1000, bytes_accessed=1000, transcendentals=0),
    )(context, wo, hidden, weight)


def shards(
    hidden,
    wq_direct,
    wkv_direct,
    wo_direct,
    kv_cache,
    parent,
    lengths,
    cand_embed,
    source,
    enc_qkv,
    enc_out,
    cross_q,
    cross_kv,
    cross_out,
    w_direct,
    w_channel,
    target_shard,
):
    dp_n, mp_n = lax.axis_size("dp"), lax.axis_size("mp")
    side_n = dp_n // mp_n
    line_n = dp_n // side_n
    me, own_mp = lax.axis_index("dp"), lax.axis_index("mp")
    side, line = me % side_n, me // side_n
    beam_n, features = hidden.shape
    span, query_n = kv_cache.shape[2], source.shape[1]
    local_width = cand_embed.shape[2]
    by_pairs = line_n == 4
    inner = (line == 1) | (line == 2)

    def move(a, pairs):
        return lax.ppermute(
            a, "dp", [(s * side_n + i, t * side_n + i) for s, t in pairs for i in range(side_n)]
        )

    def swap(a):
        return lax.ppermute(
            a, "dp", [(i, i - i % side_n + (i + 1) % side_n) for i in range(dp_n)]
        )

    def to_next(a):
        return move(a, [(0, 1), (1, 0), (2, 3), (3, 2)])

    def to_inner(a):
        return move(a, [(1, 2), (2, 1)])

    def far(own, of_next, of_inner):
        if not by_pairs:
            lines = [[k * side_n + i for k in range(line_n)] for i in range(side_n)]
            return [lax.all_gather(own, "dp", axis_index_groups=lines)]
        return [
            move(of_inner, [(1, 0), (2, 3)]),
            move(of_next, [(1, 2), (2, 1)]),
            move(of_next, [(1, 3), (2, 0)]),
        ]

    def join(of_inner, made):
        if not by_pairs:
            return made[0]
        outer, inner_last, outer_last = made
        return jnp.stack(
            [jnp.where(inner, of_inner, outer), jnp.where(inner, inner_last, outer_last)]
        )

    low = line < 2
    if by_pairs:
        places = [line, line ^ 1, jnp.where(low, 2, 1), jnp.where(low, 3, 0)]
    else:
        places = list(range(line_n))
    at = jnp.stack([side, inner, *places]).astype(jnp.int32)

    def keys_of(*stacked):
        if not by_pairs:
            sides = [[(k, place) for place in range(line_n)] for k in range(len(stacked))]
        else:
            sides = [
                [(3 * k, own), (3 * k + 1, of_next), (3 * k + 2, 0), (3 * k + 2, 1)]
                for k, (own, of_next) in enumerate(stacked)
            ]
        return sides[0] if len(sides) == 1 else list(zip(*sides, strict=True))

    def slots_of(*sides):
        return [ref for parts in sides for ref in (parts if by_pairs else parts[2:])]

    def side_part(a, of):
        width = a.shape[-1] // side_n
        return lax.dynamic_slice_in_dim(a, of * width, width, a.ndim - 1)

    def everyone(a):
        return lax.all_gather(a, "mp", axis=0)

    def exchange(a):
        return lax.all_to_all(a, "dp", split_axis=0, concat_axis=0, tiled=True)

    positions = jnp.arange(span, dtype=jnp.int32)

    def live_of(lens):
        return (positions[None, :] < lens[:, None]).astype(jnp.int32).reshape(1, -1)


    fold = cross_kv.shape[1] // enc_out.shape[0]
    qkv_sent = jnp.concatenate([side_part(w, 1 - side) for w in enc_qkv], axis=1)
    qkv_sent, enc_out, val = fence(qkv_sent, enc_out, cross_kv[1])
    qkv_got = swap(qkv_sent)
    val = jnp.concatenate(jnp.split(val, fold, axis=0), axis=1)
    qkv_own = jnp.concatenate([side_part(w, side) for w in enc_qkv], axis=1)
    out_next, val_next = (to_next(a) if by_pairs else a for a in (enc_out, val))
    out_inner, val_inner = (to_inner(a) if by_pairs else a for a in (enc_out, val))
    tokens = take_rows(cand_embed, parent, 0).reshape(beam_n * span, local_width)
    both = jnp.zeros((side_n,) + qkv_own.shape, BF16)
    both = lax.dynamic_update_index_in_dim(both, qkv_own, side, 0)
    qkv_got, out_next, val_next, out_inner, val_inner, tokens, both = fence(
        qkv_got, out_next, val_next, out_inner, val_inner, tokens, both
    )

    both = lax.dynamic_update_index_in_dim(both, qkv_got, 1 - side, 0)
    qkv_own = both.reshape(-1, both.shape[2])
    qkv_next = to_next(qkv_own) if by_pairs else qkv_own
    qkv_inner = to_inner(qkv_own) if by_pairs else qkv_own
    tokens_got = swap(tokens)
    lengths_got = swap(lengths)
    pair_next = jnp.stack([out_next, val_next])
    own_blocks = everyone(tokens)
    source_rows = lax.all_gather(source[0], "mp", axis=1, tiled=True)
    source_cut = source_rows.reshape(query_n, dp_n, -1).transpose(1, 0, 2)
    source_cut = exchange(source_cut)
    cache = take_rows(kv_cache, parent, 1)
    owns = jnp.stack([enc_out, val, cross_out])
    qkv_next, qkv_inner, tokens_got, lengths_got, owns, pair_next, cache, source_cut = fence(
        qkv_next, qkv_inner, tokens_got, lengths_got, owns, pair_next, cache, source_cut
    )

    qkv_far = far(qkv_own, qkv_next, qkv_inner)
    got_blocks = everyone(tokens_got)
    owns_cross = swap(owns)
    pair_cross = swap(pair_next) if by_pairs else pair_next
    partial = exchange(dot(source_cut.reshape(dp_n * query_n, -1), cross_q))
    live = live_of(lengths)
    context = direct_context(
        live, hidden, wq_direct, wkv_direct, cache.reshape(2, beam_n * span, -1), span
    )
    context = lax.all_gather(context, "mp", axis=1, tiled=True)
    own_start = own_mp * local_width
    hidden_share = lax.dynamic_slice_in_dim(hidden, own_start, local_width, 1)
    new_state, *sums = direct_state(context, wo_direct, hidden_share, w_direct[None])
    squares, direct_dot = lax.psum(tuple(a.reshape(-1) for a in sums), "mp")
    direct_score = direct_dot / jnp.sqrt(squares / features + EPSILON)
    (
        qkv_far,
        owns_cross,
        pair_cross,
        (out_next, out_inner, val_next, val_inner),
        last_own,
        partial,
        new_state,
        direct_score,
    ) = fence(
        qkv_far,
        owns_cross,
        pair_cross,
        (out_next, out_inner, val_next, val_inner),
        cross_out,
        partial,
        new_state,
        direct_score,
    )

    out_far = far(enc_out, out_next, out_inner)
    if by_pairs:
        qkv_keys = [(0, None), (1, None), (2, None, 3), (4, None, 5)]
        outer, inner_last, outer_last = qkv_far
        qkv_slots = [qkv_own, qkv_next, qkv_inner, outer, inner_last, outer_last]
    else:
        qkv_keys, qkv_slots = keys_of((None, None)), qkv_far
    live_got = live_of(lengths_got)
    context_got = swap(enc_attention(at, got_blocks, live_got, qkv_keys, qkv_slots, span))
    context_own = enc_attention(at, own_blocks, live, qkv_keys, qkv_slots, span)
    enc_context = jnp.stack([context_own, context_got])
    enc_context, out_far, last_own, val_next, val_inner, partial = fence(
        enc_context, out_far, last_own, val_next, val_inner, partial
    )

    enc_blocks = everyone(enc_context)
    out_far = join(out_inner, out_far)
    out_cross = swap(out_far)
    val_far = far(val, val_next, val_inner)
    queries = jnp.sum(partial.reshape(dp_n, query_n, -1), axis=0).astype(BF16)
    queries = exchange(jnp.broadcast_to(queries, (dp_n,) + queries.shape).reshape(dp_n * query_n, -1))
    enc_blocks, out_cross, val_far, last_own, queries = fence(
        enc_blocks, out_cross, val_far, last_own, queries
    )
    summed, squares = encode_out(
        at,
        enc_blocks,
        tokens,
        keys_of((None, 0), (0, 0)),
        slots_of((enc_out, pair_next, out_far), (owns_cross, pair_cross, out_cross)),
    )
    memory_blocks = everyone(summed)
    val_far = join(val_inner, val_far)
    val_cross = swap(val_far)
    last_next = to_next(last_own) if by_pairs else last_own
    last_inner = to_inner(last_own) if by_pairs else last_own
    last_next, last_inner = fence(last_next, last_inner)
    last_cross = swap(last_next) if by_pairs else last_next
    last_far = far(last_own, last_next, last_inner)
    head_n = queries.shape[1] // HD
    mixed = jnp.einsum(
        "rhc,khc->rhk",
        queries.reshape(-1, head_n, HD),
        cross_kv[0].reshape(-1, head_n, HD),
        preferred_element_type=F32,
    ).astype(BF16)
    depth = mixed.shape[2]
    pairs = head_n * query_n
    mixed = mixed.reshape(dp_n, query_n, head_n, depth).transpose(0, 2, 1, 3)
    mixed = exchange(mixed.reshape(dp_n, pairs, depth))
    mixed = mixed.reshape(line_n, side_n, pairs, depth)
    enc_squares = lax.psum(squares.reshape(1, -1), "mp").reshape(-1, 1)
    scale = 1.0 / jnp.sqrt(enc_squares / features + EPSILON)
    val_cross, last_cross, last_far, scale = fence(val_cross, last_cross, last_far, scale)
    last_far = join(last_inner, last_far)
    last_far_cross = swap(last_far)
    memory_blocks, mixed = fence(memory_blocks, mixed)

    cross_context = decode(
        at,
        memory_blocks,
        mixed,
        scale,
        live,
        keys_of((None, 1), (1, 1)),
        slots_of((val, pair_next, val_far), (owns_cross, pair_cross, val_cross)),
        span,
        query_n,
    )
    cross_blocks = everyone(cross_context)
    cross_blocks, last_far_cross = fence(cross_blocks, last_far_cross)
    dec_sums = decode_out(
        at,
        cross_blocks,
        source[0],
        w_channel[None],
        keys_of((None, None), (2, None)),
        slots_of((cross_out, last_next, last_far), (owns_cross, last_cross, last_far_cross)),
    )
    dec_squares, dec_dot = lax.psum(tuple(a.reshape(1, -1) for a in dec_sums), "mp")
    position_score = dec_dot / jnp.sqrt(dec_squares / features + EPSILON)
    own_channel = jnp.mean(position_score.reshape(beam_n, query_n), axis=1)
    shard_ids = lax.broadcasted_iota(jnp.int32, (dp_n, beam_n), 0)
    sent_scores = jnp.where(shard_ids == target_shard[None], own_channel[None], 0.0)
    return (new_state, direct_score + own_channel, jnp.sum(exchange(sent_scores), axis=0))


def solution(mesh):
    in_specs = (
        P("dp", None),
        P(None, "mp"),
        P(None, None, "mp"),
        P(None, "mp"),
        P(None, "dp", None, "mp"),
        P("dp"),
        P("dp"),
        P("dp", None, "mp"),
        P("dp", None, "mp"),
        P(None, "dp", "mp"),
        P("dp", "mp"),
        P("dp", "mp"),
        P(None, "dp", "mp"),
        P("dp", "mp"),
        P("mp"),
        P("mp"),
        P("dp"),
    )
    out_specs = (P("dp", "mp"), P("dp"), P("dp"))
    return jax.shard_map(shards, mesh=mesh, in_specs=in_specs, out_specs=out_specs, check_vma=False)
```
